256 devices in a mesh: grp: 16 (over x_lo, z), blk: 16 (over y, x_hi, core).
Axes of the slice: x: 4 (x_hi: 2, x_lo: 2; x = x_hi * 2 + x_lo), y: 4, z: 8, core: 2. Of those that a mesh axis runs over, the one named last changes fastest.
Arguments:
- image_emb: bfloat16 [32768, 1152], P(('grp', 'blk')), may hold values from -6 to 6
- text_hidden: bfloat16 [32768, 4304], P(('grp', 'blk')), may hold values from -6 to 6
- head_weight: bfloat16 [4304, 1152], replicated, may hold values from -0.09375 to 0.09375
- positive: int32 [256, 128], P(('grp', 'blk')), may hold values from 0 to 127, each once within a row
- log_scale: float32 [1], replicated, may hold values from 4 to 4.5
- bias: float32 [1], replicated, may hold values from -9 to -6
Outputs:
- image_grad: float32 [32768, 1152], P(('grp', 'blk'))
- head_grad: float32 [4304, 1152], P('blk', 'grp')
The draws below stay inside these ranges and needn't reach their ends.
Inputs may be any that keep to these rules, and one draw needn't show every extreme that they name: Each row of positive is a permutation of the 128 rows of one device: image r of a device is paired with text positive[., r] of the same device.
All inputs are finite; a program needn't handle non-finite values.
Results may differ from the reference program's by a relative error of at most 0.038.
Values may be sent and summed in bfloat16 or wider, within the bound.
A program may use at most 64 MiB of HBM per device.

```python
import jax
import jax.numpy as jnp
from jax import lax

D = 1152
FF = 4304
TOK_DEV = 128
TOKENS = 32768
N_GRP = 16
N_BLK = 16


def block_scale(stream_key, extent, cuts, low, top_value):
    level = 1.0
    for position, parts in cuts:
        draws = jax.random.uniform(jax.random.fold_in(jax.random.fold_in(stream_key, 6), position), (parts,), jnp.float32, low / len(cuts), top_value / len(cuts))
        level = level * jnp.repeat(jnp.exp(draws), extent[position] // parts).reshape((-1,) + (1,) * (len(extent) - 1 - position))
    return level


def noise(key, extent, width, reach, cuts=(), held_as=jnp.bfloat16):
    values = width * jax.random.normal(key, extent, jnp.float32)
    if cuts:
        values = values * block_scale(key, extent, cuts, -0.22, 0.18)
    return jnp.clip(values, -reach, reach).astype(held_as)


def setup_inputs(seed: int = 0) -> dict:
    arg_keys = jax.random.split(jax.random.key(seed), 7)
    image_emb = noise(arg_keys[0], (TOKENS, D), 1.0, 6.0, ((0, 256),))
    text_hidden = noise(arg_keys[1], (TOKENS, FF), 1.0, 6.0, ((0, 256),))
    head_weight = noise(arg_keys[2], (FF, D), FF ** -0.5, 0.09375)
    positive = jax.vmap(lambda own: jax.random.permutation(own, TOK_DEV))(jax.random.split(arg_keys[3], (N_GRP * N_BLK))).reshape((N_GRP * N_BLK, TOK_DEV)).astype(jnp.int32)
    log_scale = jnp.clip(jax.random.uniform(arg_keys[4], (1,), jnp.float32, 4.0, 4.5), 4.0, 4.5)
    bias = jnp.clip(jax.random.uniform(arg_keys[5], (1,), jnp.float32, -9.0, -6.0), -9.0, -6.0)
    return {"image_emb": image_emb, "text_hidden": text_hidden, "head_weight": head_weight, "positive": positive, "log_scale": log_scale, "bias": bias}


def normalize(raw_values):
    norm_value = jnp.sqrt(lax.optimization_barrier(jnp.sum(raw_values * raw_values, axis=-1, keepdims=True)) + 1e-06)
    return (norm_value, raw_values / norm_value)

def unit_back(direction, incoming, norm_value):
    along = lax.optimization_barrier(jnp.sum(direction * incoming, axis=-1, keepdims=True))
    return (incoming - direction * along) / norm_value

def reference(image_emb, text_hidden, head_weight, positive, log_scale, bias):
    group_rows = TOK_DEV * N_BLK
    images = image_emb.reshape(N_GRP, group_rows, D)
    hidden = text_hidden.reshape(N_GRP, group_rows, FF)
    pos_groups = positive.reshape(N_GRP, N_BLK, TOK_DEV)
    logit_scale = jnp.exp(log_scale[0])
    logit_bias = bias[0]

    def per_group(head_sum, inputs):
        image_rows, hidden_rows, pos_group = inputs
        image_norm, image_dir = normalize(image_rows.astype(jnp.float32))
        image_unit = image_dir.astype(jnp.bfloat16)
        text_raw = jnp.dot(hidden_rows, head_weight, preferred_element_type=jnp.float32)
        text_norm, text_dir = normalize(text_raw)
        text_unit = text_dir.astype(jnp.bfloat16)
        logits = logit_scale * jnp.dot(image_unit, text_unit.T, preferred_element_type=jnp.float32) + logit_bias
        offsets = (jnp.arange(N_BLK, dtype=jnp.int32) * TOK_DEV)[:, None]
        target = (offsets + pos_group).reshape(group_rows)
        columns = jnp.arange(group_rows, dtype=jnp.int32)
        labels = (target[:, None] == columns[None, :]).astype(jnp.float32)
        weight = (logit_scale * (jax.nn.sigmoid(logits) - labels)).astype(jnp.bfloat16)
        image_dir_grad = jnp.dot(weight, text_unit, preferred_element_type=jnp.float32)
        text_dir_grad = jnp.dot(weight.T, image_unit, preferred_element_type=jnp.float32)
        image_grad = unit_back(image_dir, image_dir_grad, image_norm)
        text_raw_grad = unit_back(text_dir, text_dir_grad, text_norm).astype(jnp.bfloat16)

        def block(running, pieces):
            hidden_block, grad_block = pieces
            head_part = jnp.dot(hidden_block.T, grad_block, preferred_element_type=jnp.float32)
            rounded = lax.optimization_barrier(head_part.astype(jnp.bfloat16))
            return (running + rounded.astype(jnp.float32), None)
        head_sum, _ = lax.scan(block, head_sum, (hidden_rows.reshape(N_BLK, TOK_DEV, FF), text_raw_grad.reshape(N_BLK, TOK_DEV, D)))
        return (head_sum, image_grad)
    head_grad, image_grads = lax.scan(per_group, jnp.zeros((FF, D), jnp.float32), (images, hidden, pos_groups))
    return (image_grads.reshape(N_GRP * group_rows, D), head_grad)
```

```python
import functools

import jax
import jax.numpy as jnp
from jax import lax
from jax.experimental import pallas as pl
from jax.experimental.pallas import tpu as pltpu
from jax.sharding import PartitionSpec as P

MESH = pl.DeviceIdType.MESH
BF16 = jnp.bfloat16
F32 = jnp.float32

ROWS = 128
D = 1152
FF = 4304
FF_DEV = 269
FF_PAD = 272
D_DEV = 72
HALF = 640
CHUNK = 512
HALF_ROWS = ROWS // 2
N_SENDS = 19


def nt_dot(left, right):
    return lax.dot_general(left, right, (((1,), (1,)), ((), ())), preferred_element_type=F32)


class Place:
    def __init__(self):
        self.g = lax.axis_index("grp")
        self.b = lax.axis_index("blk")
        y, rest = lax.div(self.b, 4), lax.rem(self.b, 4)
        xh, self.c = lax.div(rest, 2), lax.rem(rest, 2)

        def at(dy, flip_x, flip_c):
            x = 1 - xh if flip_x else xh
            c = 1 - self.c if flip_c else self.c
            return lax.rem(y + dy, 4) * 4 + x * 2 + c

        self.at = at
        self.chip = lambda dy, flip_x: lax.rem(y + dy, 4) * 2 + (1 - xh if flip_x else xh)
        self.xl, self.z = lax.div(self.g, 8), lax.rem(self.g, 8)


FULL, LOW, HIGH = (0, ROWS), (0, HALF_ROWS), (HALF_ROWS, HALF_ROWS)
UP, DOWN, ACROSS, TWIN = (1, 0, 0), (3, 0, 0), (0, 1, 0), (0, 0, 1)
SENDS = [
    ((0, 0, 0), FULL, ACROSS, (0, 1, 0)),
    ((0, 0, 0), FULL, UP, (3, 0, 0)),
    ((0, 0, 0), FULL, DOWN, (1, 0, 0)),
    ((3, 0, 0), LOW, UP, (2, 0, 0)),
    ((1, 0, 0), HIGH, DOWN, (2, 0, 0)),
    ((0, 1, 0), FULL, UP, (3, 1, 0)),
    ((0, 1, 0), FULL, DOWN, (1, 1, 0)),
    ((3, 1, 0), LOW, UP, (2, 1, 0)),
    ((1, 1, 0), HIGH, DOWN, (2, 1, 0)),
    ((0, 0, 0), FULL, TWIN, (0, 0, 1)),
    ((0, 1, 0), FULL, TWIN, (0, 1, 1)),
    ((3, 0, 0), FULL, TWIN, (3, 0, 1)),
    ((1, 0, 0), FULL, TWIN, (1, 0, 1)),
    ((3, 1, 0), FULL, TWIN, (3, 1, 1)),
    ((1, 1, 0), FULL, TWIN, (1, 1, 1)),
    ((2, 0, 0), LOW, TWIN, (2, 0, 1)),
    ((2, 0, 0), HIGH, TWIN, (2, 0, 1)),
    ((2, 1, 0), LOW, TWIN, (2, 1, 1)),
    ((2, 1, 0), HIGH, TWIN, (2, 1, 1)),
]


class Gather:
    def __init__(self, place, buf, send_sem, recv_sem):
        self.place, self.buf, self.send_sem, self.recv_sem = place, buf, send_sem, recv_sem
        self.held = []

    def copy(self, i, block):
        _, (first, count), target, _ = SENDS[i]
        ref = self.buf.at[self.place.at(*block), pl.ds(first, count)]
        return pltpu.make_async_remote_copy(
            src_ref=ref,
            dst_ref=ref,
            send_sem=self.send_sem.at[i],
            recv_sem=self.recv_sem.at[i],
            device_id=(self.place.g, self.place.at(*target)),
            device_id_type=MESH,
        )

    def send(self, *which):
        for i in which:
            copy = self.copy(i, SENDS[i][0])
            copy.start()
            self.held.append(copy)

    def got(self, *which):
        for i in which:
            self.copy(i, SENDS[i][3]).wait_recv()

    def start(self):
        self.send(0, 1, 2, 9)

    def stage_a(self):
        self.got(1)
        self.send(3, 11)
        self.got(2)
        self.send(4, 12)

    def stage_b(self):
        self.got(0)
        self.send(5, 6, 10)

    def stage_c(self):
        self.got(3)
        self.send(15)
        self.got(4)
        self.send(16)

    def stage_d(self):
        self.got(5)
        self.send(7, 13)
        self.got(6)
        self.send(8, 14)

    def stage_e(self):
        self.got(7)
        self.send(17)
        self.got(8)
        self.send(18)

    def finish(self):
        for copy in self.held:
            copy.wait_send()


ORDER = [
    ((0, 0), (9,)),
    ((3, 0), (11,)),
    ((1, 0), (12,)),
    ((0, 1), (10,)),
    ((2, 0), (15, 16)),
    ((3, 1), (13,)),
    ((1, 1), (14,)),
    ((2, 1), (17, 18)),
]


def kernel(
    image_ref, hidden_ref, weight_ref, positive_ref, scale_ref, bias_ref,
    image_out, head_out,
    weight_buf, images, texts, grads, raw, text_sum, image_sum,
    piece_out, piece_in, head, head_half, half_in, part_out, part_in,
    weight_sem, img_send, img_recv, txt_send, txt_recv, grd_send, grd_recv,
    hid_send, hid_recv, half_sem, part_send, part_recv,
):
    place = Place()
    g, b, c, xl, z = place.g, place.b, place.c, place.xl, place.z

    barrier = pltpu.get_barrier_semaphore()
    for d in range(1, 16):
        pl.semaphore_signal(barrier, inc=1, device_id=(g, lax.rem(b + d, 16)), device_id_type=MESH)
    other_half = (1 - xl) * 8 + z
    pl.semaphore_signal(barrier, inc=1, device_id=(other_half, b), device_id_type=MESH)
    for d in range(1, 8):
        peer = xl * 8 + lax.rem(z + d, 8)
        pl.semaphore_signal(barrier, inc=1, device_id=(peer, b), device_id_type=MESH)

    bounds = [(k, min(CHUNK, FF - k)) for k in range(0, FF, CHUNK)]
    weight_copies = []
    for n, (first, count) in enumerate(bounds):
        rows = pl.ds(first, count)
        copy = pltpu.make_async_copy(weight_ref.at[rows], weight_buf.at[rows], weight_sem.at[n])
        copy.start()
        weight_copies.append(copy)

    def unit_of(values):
        norm = jnp.sqrt(jnp.sum(values * values, axis=-1, keepdims=True) + 1e-06)
        return norm, values / norm

    def unit_back(values, incoming):
        norm, direction = unit_of(values)
        along = jnp.sum(direction * incoming, axis=-1, keepdims=True)
        return (incoming - direction * along) / norm

    images[b] = unit_of(image_ref[...].astype(F32))[1].astype(BF16)
    pl.semaphore_wait(barrier, 23)

    img = Gather(place, images, img_send, img_recv)
    txt = Gather(place, texts, txt_send, txt_recv)
    grd = Gather(place, grads, grd_send, grd_recv)
    img.start()

    between = {3: img.stage_a, 5: img.stage_b, 6: img.stage_c, 8: img.stage_d}
    for n, (first, count) in enumerate(bounds):
        weight_copies[n].wait()
        term = jnp.dot(
            hidden_ref[:, first : first + count],
            weight_buf[first : first + count],
            preferred_element_type=F32,
        )
        raw[...] = term if n == 0 else raw[...] + term
        if n in between:
            between[n]()
    texts[b] = unit_of(raw[...])[1].astype(BF16)

    def cut(first, window, shift):
        row = lax.broadcasted_iota(jnp.int32, (FF_PAD, window), 0)
        column = lax.broadcasted_iota(jnp.int32, (FF_PAD, window), 1)
        pick = jnp.where(column == row + shift, 1.0, 0.0).astype(BF16)
        return nt_dot(pick, hidden_ref[:, pl.ds(first, window)]).astype(BF16)

    def cut_step(n, carry):
        start = n * FF_DEV
        first = pl.multiple_of(lax.div(start, 128) * 128, 128)
        piece_out[n] = cut(first, 512, start - first)
        return carry

    lax.fori_loop(0, 15, cut_step, 0)
    last = 15 * FF_DEV
    piece_out[15] = cut(last // 128 * 128, FF - last // 128 * 128, last % 128)
    img.stage_e()

    pair, lane = lax.div(b, 2), pl.multiple_of(c * 128, 128)
    piece_in[pair, :, pl.ds(lane, 128)] = piece_out[b]

    def piece_copy(d, target, sender):
        return pltpu.make_async_remote_copy(
            src_ref=piece_out.at[target],
            dst_ref=piece_in.at[lax.div(sender, 2), :, pl.ds(pl.multiple_of(lax.rem(sender, 2) * 128, 128), 128)],
            send_sem=hid_send.at[d - 1],
            recv_sem=hid_recv.at[d - 1],
            device_id=(g, target),
            device_id_type=MESH,
        )

    for d in range(1, 16):
        piece_copy(d, lax.rem(b + d, 16), b).start()

    logit_scale = jnp.exp(scale_ref[...])
    logit_bias = bias_ref[...]
    text_row = lax.broadcasted_iota(jnp.int32, (ROWS, ROWS), 0)
    label = jnp.where(text_row == positive_ref[...], 1.0, 0.0)

    def with_twin(own):
        return jnp.concatenate([jnp.where(c == 0, own, 0.0), jnp.where(c == 0, 0.0, own)], axis=1)

    def visit(unit, others, chip, total, own_label=None):
        block = others[pl.ds(2 * chip, 2)].reshape(2 * ROWS, D)
        chance = jax.nn.sigmoid(logit_scale * nt_dot(unit, block) + logit_bias)
        if own_label is not None:
            chance = chance - with_twin(own_label)
        weight = (logit_scale * chance).astype(BF16)
        term = jnp.dot(weight, block, preferred_element_type=F32)
        total[...] = term if own_label is not None else total[...] + term

    for n, (where, twins) in enumerate(ORDER):
        img.got(*twins)
        visit(texts[b], images, place.chip(*where), text_sum, label if n == 0 else None)

    grads[b] = unit_back(raw[...], text_sum[...]).astype(BF16)
    grd.start()

    for d in range(1, 16):
        piece_copy(d, lax.rem(b + d, 16), lax.rem(b + 16 - d, 16)).wait_recv()

    def add_head(n):
        where, twins = ORDER[n]
        grd.got(*twins)
        chip = place.chip(*where)
        block = grads[pl.ds(2 * chip, 2)].reshape(2 * ROWS, D)
        term = jnp.dot(piece_in[chip], block, preferred_element_type=F32)
        head[...] = term if n == 0 else head[...] + term

    add_head(0)
    grd.stage_a()
    grd.stage_b()
    add_head(1)
    add_head(2)
    grd.stage_c()
    grd.stage_d()
    add_head(3)
    add_head(4)
    txt.start()
    grd.stage_e()
    add_head(5)
    add_head(6)
    add_head(7)

    head_half[...] = head[:, pl.ds(pl.multiple_of((1 - xl) * 512, 128), HALF)].astype(BF16)
    half_copy = pltpu.make_async_remote_copy(
        src_ref=head_half,
        dst_ref=half_in,
        send_sem=half_sem.at[0],
        recv_sem=half_sem.at[1],
        device_id=(other_half, b),
        device_id_type=MESH,
    )
    half_copy.start()
    txt.stage_a()
    txt.got(9)
    visit(images[b], texts, place.chip(0, 0), image_sum, jnp.transpose(label))
    half_copy.wait_recv()
    mine = head[:, pl.ds(pl.multiple_of(xl * 512, 128), HALF)] + half_in[...].astype(F32)
    head[:, 0:HALF] = mine
    row = lax.broadcasted_iota(jnp.int32, (256, 128), 0)
    column = lax.broadcasted_iota(jnp.int32, (256, 128), 1)
    for n in range(8):
        first = n * D_DEV // 128 * 128
        shift = n * D_DEV % 128
        pick = jnp.where((row == column + shift + 64 * xl) & (column < D_DEV), 1.0, 0.0).astype(BF16)
        part_out[n] = jnp.dot(
            head[:, first : first + 256].astype(BF16), pick, preferred_element_type=F32
        ).astype(BF16)

    def part_copy(d):
        target = lax.rem(z + d, 8)
        return pltpu.make_async_remote_copy(
            src_ref=part_out.at[target],
            dst_ref=part_in.at[d - 1],
            send_sem=part_send.at[d - 1],
            recv_sem=part_recv.at[d - 1],
            device_id=(xl * 8 + target, b),
            device_id_type=MESH,
        )

    for d in range(1, 8):
        part_copy(d).start()

    txt.stage_b()
    txt.stage_c()
    txt.stage_d()
    for n in range(1, 5):
        where, twins = ORDER[n]
        txt.got(*twins)
        visit(images[b], texts, place.chip(*where), image_sum)
    txt.stage_e()
    for n in range(5, 8):
        where, twins = ORDER[n]
        txt.got(*twins)
        visit(images[b], texts, place.chip(*where), image_sum)
    image_out[...] = unit_back(image_ref[...].astype(F32), image_sum[...])

    total = part_out[z].astype(F32)
    for d in range(1, 8):
        part_copy(d).wait_recv()
        total = total + part_in[d - 1].astype(F32)
    head_out[...] = total[:FF_DEV, :D_DEV]

    img.finish()
    txt.finish()
    grd.finish()
    for d in range(1, 16):
        piece_copy(d, lax.rem(b + d, 16), b).wait_send()
    for d in range(1, 8):
        part_copy(d).wait_send()
    half_copy.wait_send()


def local(image_emb, text_hidden, head_weight, positive, log_scale, bias):
    vmem = pl.BlockSpec(memory_space=pltpu.VMEM)
    dma = pltpu.SemaphoreType.DMA
    return pl.pallas_call(
        kernel,
        out_shape=(
            jax.ShapeDtypeStruct((ROWS, D), F32),
            jax.ShapeDtypeStruct((FF_DEV, D_DEV), F32),
        ),
        in_specs=[vmem, vmem, pl.BlockSpec(memory_space=pl.ANY), vmem, vmem, vmem],
        out_specs=(vmem, vmem),
        scratch_shapes=[
            pltpu.VMEM((FF, D), BF16),
            pltpu.VMEM((16, ROWS, D), BF16),
            pltpu.VMEM((16, ROWS, D), BF16),
            pltpu.VMEM((16, ROWS, D), BF16),
            pltpu.VMEM((ROWS, D), F32),
            pltpu.VMEM((ROWS, D), F32),
            pltpu.VMEM((ROWS, D), F32),
            pltpu.VMEM((16, FF_PAD, ROWS), BF16),
            pltpu.VMEM((8, FF_PAD, 2 * ROWS), BF16),
            pltpu.VMEM((FF_PAD, D), F32),
            pltpu.VMEM((FF_PAD, HALF), BF16),
            pltpu.VMEM((FF_PAD, HALF), BF16),
            pltpu.VMEM((8, FF_PAD, 128), BF16),
            pltpu.VMEM((7, FF_PAD, 128), BF16),
            dma((9,)),
            dma((N_SENDS,)),
            dma((N_SENDS,)),
            dma((N_SENDS,)),
            dma((N_SENDS,)),
            dma((N_SENDS,)),
            dma((N_SENDS,)),
            dma((15,)),
            dma((15,)),
            dma((2,)),
            dma((7,)),
            dma((7,)),
        ],
        compiler_params=pltpu.CompilerParams(
            collective_id=0, has_side_effects=True, vmem_limit_bytes=60 * 1024 * 1024
        ),
    )(
        image_emb,
        text_hidden,
        head_weight,
        positive,
        log_scale.reshape(1, 1),
        bias.reshape(1, 1),
    )


def solution(mesh):
    in_specs = (
        P(("grp", "blk"), None),
        P(("grp", "blk"), None),
        P(),
        P(("grp", "blk"), None),
        P(),
        P(),
    )
    out_specs = (P(("grp", "blk"), None), P("blk", "grp"))
    return jax.shard_map(local, mesh=mesh, in_specs=in_specs, out_specs=out_specs, check_vma=False)
```

```python
import jax
import jax.numpy as jnp
from jax import lax
from jax.experimental import pallas as pl
from jax.experimental.pallas import tpu as pltpu
from jax.sharding import PartitionSpec as P

MESH = pl.DeviceIdType.MESH
BF16 = jnp.bfloat16
F32 = jnp.float32

ROWS = 128
D = 1152
FF = 4304
FF_DEV = 269
FF_PAD = 272
WINDOW = 288
D_DEV = 72
LANES = 640
CHUNK = 512
FIRST_ROWS = 128


def nt_dot(left, right):
    return lax.dot_general(left, right, (((1,), (1,)), ((), ())), preferred_element_type=F32)


def tn_dot(left, right):
    return lax.dot_general(left, right, (((0,), (0,)), ((), ())), preferred_element_type=F32)


class Place:
    def __init__(self):
        self.g = lax.axis_index("grp")
        self.b = lax.axis_index("blk")
        rest = lax.rem(self.b, 4)
        self.y, self.xh, self.c = lax.div(self.b, 4), lax.div(rest, 2), lax.rem(rest, 2)
        self.xl, self.z = lax.div(self.g, 8), lax.rem(self.g, 8)

    def slot(self, dy, flip_c):
        return self.turn(dy) * 2 + (1 - self.c if flip_c else self.c)

    def turn(self, dy):
        return lax.rem(self.y + dy, 4)

    def device(self, dy=0, flip_c=0, flip_xh=0, flip_xl=0, dz=0):
        c = 1 - self.c if flip_c else self.c
        xh = 1 - self.xh if flip_xh else self.xh
        xl = 1 - self.xl if flip_xl else self.xl
        return (xl * 8 + lax.rem(self.z + dz, 8), self.turn(dy) * 4 + xh * 2 + c)


FULL, LOW, HIGH = (0, ROWS), (0, ROWS // 2), (ROWS // 2, ROWS // 2)
OWN, UP, DOWN, FAR, TWIN = (0, 0), (1, 0), (3, 0), (2, 0), (0, 1)
SENDS = [
    (OWN, LOW, UP, DOWN),
    (OWN, HIGH, DOWN, UP),
    (OWN, HIGH, UP, DOWN),
    (OWN, LOW, DOWN, UP),
    (DOWN, LOW, UP, FAR),
    (UP, HIGH, DOWN, FAR),
    (OWN, FULL, TWIN, TWIN),
    (DOWN, FULL, TWIN, (3, 1)),
    (UP, FULL, TWIN, (1, 1)),
    (FAR, LOW, TWIN, (2, 1)),
    (FAR, HIGH, TWIN, (2, 1)),
]
ORDER = [(0, (6,)), (3, (7,)), (1, (8,)), (2, (9, 10))]


class Gather:
    def __init__(self, place, buf, send_sem, recv_sem):
        self.place, self.buf, self.send_sem, self.recv_sem = place, buf, send_sem, recv_sem
        self.held = []

    def copy(self, i, block):
        _, (first, count), target, _ = SENDS[i]
        ref = self.buf.at[self.place.slot(*block), pl.ds(first, count)]
        return pltpu.make_async_remote_copy(
            src_ref=ref,
            dst_ref=ref,
            send_sem=self.send_sem.at[i],
            recv_sem=self.recv_sem.at[i],
            device_id=self.place.device(*target),
            device_id_type=MESH,
        )

    def send(self, *which):
        for i in which:
            copy = self.copy(i, SENDS[i][0])
            copy.start()
            self.held.append(copy)

    def got(self, *which):
        for i in which:
            self.copy(i, SENDS[i][3]).wait_recv()

    def start(self):
        self.send(0, 1, 2, 3, 6)

    def pass_on(self):
        self.got(0)
        self.send(4)
        self.got(1)
        self.send(5)

    def near(self):
        self.got(2)
        self.send(7)
        self.got(3)
        self.send(8)

    def far(self):
        self.got(4)
        self.send(9)
        self.got(5)
        self.send(10)

    def finish(self):
        for copy in self.held:
            copy.wait_send()


def kernel(
    image_ref, hidden_ref, weight_ref, positive_ref, scale_ref, bias_ref,
    image_out, head_out,
    weight_buf, images, texts, grads, image_far, text_far, raw,
    text_sum, image_sum, far_sum, text_back_out, text_back_in, image_back_out, image_back_in,
    piece_out, piece_in, head, head_out16, head_in, turned, part_a, part_b, in_a, in_b,
    weight_sem, img_send, img_recv, txt_send, txt_recv, grd_send, grd_recv,
    x_send, x_recv, hid_send, hid_recv, half_send, half_recv, part_send, part_recv,
):
    place = Place()
    y, c, xh, xl, z = place.y, place.c, place.xh, place.xl, place.z
    own = place.slot(*OWN)

    barrier = pltpu.get_barrier_semaphore()
    peers = [place.device(dy, fc) for dy in range(4) for fc in range(2) if dy or fc]
    peers += [place.device(flip_xh=1), place.device(flip_xl=1), place.device(flip_xh=1, flip_xl=1)]
    peers += [place.device(dz=d) for d in range(1, 8)]
    for peer in peers:
        pl.semaphore_signal(barrier, inc=1, device_id=peer, device_id_type=MESH)

    bounds = [(k, min(CHUNK, FF - k)) for k in range(0, FF, CHUNK)]
    weight_copies = []
    for n, (first, count) in enumerate(bounds):
        rows = pl.ds(first, count)
        copy = pltpu.make_async_copy(weight_ref.at[rows], weight_buf.at[rows], weight_sem.at[n])
        copy.start()
        weight_copies.append(copy)

    def unit_of(values):
        norm = jnp.sqrt(jnp.sum(values * values, axis=-1, keepdims=True) + 1e-06)
        return norm, values / norm

    def unit_back(values, incoming):
        norm, direction = unit_of(values)
        along = jnp.sum(direction * incoming, axis=-1, keepdims=True)
        return (incoming - direction * along) / norm

    def across(n, src, dst):
        return pltpu.make_async_remote_copy(
            src_ref=src,
            dst_ref=dst,
            send_sem=x_send.at[n],
            recv_sem=x_recv.at[n],
            device_id=place.device(flip_xh=1),
            device_id_type=MESH,
        )

    img = Gather(place, images, img_send, img_recv)
    txt = Gather(place, texts, txt_send, txt_recv)
    grd = Gather(place, grads, grd_send, grd_recv)
    image_across = across(0, images.at[own], image_far)
    text_across = across(1, texts.at[own], text_far)
    text_back = across(2, text_back_out, text_back_in)
    image_back = across(3, image_back_out, image_back_in)

    def begin():
        images[own] = unit_of(image_ref[...].astype(F32))[1].astype(BF16)
        pl.semaphore_wait(barrier, len(peers))
        img.start()
        image_across.start()

    between = {1: begin, 8: img.pass_on}
    for n, (first, count) in enumerate(bounds):
        weight_copies[n].wait()
        rows = pl.ds(first, count)
        term = tn_dot(hidden_ref[rows], weight_buf[rows])
        raw[...] = term if n == 0 else raw[...] + term
        if n in between:
            between[n]()
    texts[own] = unit_of(raw[...])[1].astype(BF16)
    text_across.start()
    img.near()

    def cut(start, first, window):
        row = lax.broadcasted_iota(jnp.int32, (FF_PAD, window), 0)
        column = lax.broadcasted_iota(jnp.int32, (FF_PAD, window), 1)
        pick = jnp.where(column == row + (start - first), 1.0, 0.0).astype(BF16)
        return jnp.dot(
            pick, hidden_ref[pl.ds(first, window)], preferred_element_type=F32
        ).astype(BF16)

    def cut_step(n, carry):
        start = n * FF_DEV
        first = pl.multiple_of(lax.div(start, 16) * 16, 16)
        column, half = lax.div(n, 4) * 2 + lax.rem(n, 2), lax.rem(lax.div(n, 2), 2)
        rows = pl.ds(pl.multiple_of(half * FF_PAD, 16), FF_PAD)
        piece_out[column, rows] = cut(start, first, WINDOW)
        return carry

    lax.fori_loop(0, 15, cut_step, 0)
    last = 15 * FF_DEV
    piece_out[7, FF_PAD : 2 * FF_PAD] = cut(last, last // 16 * 16, FF - last // 16 * 16)

    def lane(core):
        return pl.ds(pl.multiple_of(core * ROWS, ROWS), ROWS)

    OTHERS = [(dy, fc) for dy in (1, 3, 2) for fc in range(2)] + [TWIN]

    def piece_copy(n, dy, fc, back=False):
        if back:
            dst = piece_in.at[place.turn(4 - dy), :, lane(1 - c if fc else c)]
        else:
            dst = piece_in.at[y, :, lane(c)]
        return pltpu.make_async_remote_copy(
            src_ref=piece_out.at[place.slot(dy, fc)],
            dst_ref=dst,
            send_sem=hid_send.at[n],
            recv_sem=hid_recv.at[n],
            device_id=place.device(dy, fc),
            device_id_type=MESH,
        )

    pieces = [piece_copy(n, *target) for n, target in enumerate(OTHERS)]
    for copy in pieces:
        copy.start()
    piece_in[y, :, lane(c)] = piece_out[own]
    img.far()

    logit_scale = jnp.exp(scale_ref[...])
    logit_bias = bias_ref[...]
    text_row = lax.broadcasted_iota(jnp.int32, (ROWS, ROWS), 0)
    label = jnp.where(text_row == positive_ref[...], 1.0, 0.0)

    def with_twin(value):
        return jnp.concatenate(
            [jnp.where(c == 0, value, 0.0), jnp.where(c == 0, 0.0, value)], axis=1
        )

    def chip(buf, dy):
        return buf[pl.ds(2 * place.turn(dy), 2)].reshape(2 * ROWS, D)

    def visit(unit, block, total, first, own_label=None):
        chance = jax.nn.sigmoid(logit_scale * nt_dot(unit, block) + logit_bias)
        if own_label is not None:
            chance = chance - with_twin(own_label)
        weight = (logit_scale * chance).astype(BF16)
        term = jnp.dot(weight, block, preferred_element_type=F32)
        total[...] = term if first else total[...] + term

    for n, (dy, twins) in enumerate(ORDER):
        img.got(*twins)
        visit(texts[own], chip(images, dy), text_sum, n == 0, label if n == 0 else None)
    text_across.wait_recv()
    for n, (dy, _) in enumerate(ORDER):
        visit(text_far[...], chip(images, dy), far_sum, n == 0)
    text_back_out[...] = far_sum[...].astype(BF16)
    text_back.start()
    for n, (dy, fc) in enumerate(OTHERS):
        piece_copy(n, dy, fc, back=True).wait_recv()
    text_back.wait_recv()
    incoming = text_sum[...] + text_back_in[...].astype(F32)
    grads[own] = unit_back(raw[...], incoming).astype(BF16)
    grd.start()

    def add_head(dy, n):
        term = jnp.dot(piece_in[place.turn(dy)], chip(grads, dy), preferred_element_type=F32)
        head[...] = term if n == 0 else head[...] + term

    grd.got(6)
    add_head(0, 0)
    grd.pass_on()
    txt.start()
    grd.near()
    grd.got(7)
    add_head(3, 1)
    grd.got(8)
    add_head(1, 2)
    grd.far()
    grd.got(9, 10)
    add_head(2, 3)
    head_out16[...] = head[...].astype(BF16)

    PARTS = [(0, FIRST_ROWS), (FIRST_ROWS, FF_PAD - FIRST_ROWS)]
    FLIPS = [(0, 1), (1, 0), (1, 1)]

    def half_copy(n, flips, part):
        flip_xh, flip_xl = flips
        first, count = PARTS[part]
        to_xh = 1 - xh if flip_xh else xh
        to_xl = 1 - xl if flip_xl else xl
        rows = pl.ds(pl.multiple_of(to_xh * FF_PAD + first, 16), count)
        lanes = pl.ds(pl.multiple_of(to_xl * 512, 128), LANES)
        return pltpu.make_async_remote_copy(
            src_ref=head_out16.at[rows, lanes],
            dst_ref=head_in.at[n, pl.ds(first, count)],
            send_sem=half_send.at[part * 3 + n],
            recv_sem=half_recv.at[part * 3 + n],
            device_id=place.device(flip_xh=flip_xh, flip_xl=flip_xl),
            device_id_type=MESH,
        )

    halves = [[half_copy(n, flips, part) for n, flips in enumerate(FLIPS)] for part in range(2)]
    for copy in halves[0]:
        copy.start()
    txt.pass_on()
    for copy in halves[0]:
        copy.wait_send()
    for copy in halves[1]:
        copy.start()
    txt.near()

    def summed(part):
        first, count = PARTS[part]
        for copy in halves[part]:
            copy.wait_recv()
        rows = pl.ds(pl.multiple_of(xh * FF_PAD + first, 16), count)
        total = head[rows, pl.ds(pl.multiple_of(xl * 512, 128), LANES)]
        for n in range(3):
            total = total + head_in[n, first : first + count].astype(F32)
        return total

    def turned_rows(n):
        return pl.ds(pl.multiple_of(n * D_DEV + xl * 64, 8), D_DEV)

    def part_copy(d, part):
        target = lax.rem(z + d, 8)
        src, dst = ((part_a, in_a), (part_b, in_b))[part]
        return pltpu.make_async_remote_copy(
            src_ref=src.at[target],
            dst_ref=dst.at[d - 1],
            send_sem=part_send.at[part * 7 + d - 1],
            recv_sem=part_recv.at[part * 7 + d - 1],
            device_id=place.device(dz=d),
            device_id_type=MESH,
        )

    ROUND = (1, 7, 2, 6, 3, 5, 4)
    parts = [[part_copy(d, part) for d in ROUND] for part in range(2)]

    turned[...] = jnp.transpose(summed(0))
    for n in range(8):
        part_a[n, 0:D_DEV] = turned[turned_rows(n)].astype(BF16)
    for copy in parts[0]:
        copy.start()

    txt.got(6)
    visit(images[own], chip(texts, 0), image_sum, True, jnp.transpose(label))
    total = summed(1)
    turned[...] = jnp.transpose(total[0:128])
    row = lax.broadcasted_iota(jnp.int32, (256, 128), 0)
    column = lax.broadcasted_iota(jnp.int32, (256, 128), 1)
    rest = total[128:144].astype(BF16)
    for n in range(8):
        part_b[n, 0:D_DEV] = turned[turned_rows(n)].astype(BF16)
        first = min(n * D_DEV // 128 * 128, LANES - 256)
        shift = n * D_DEV - first + 64 * xl
        pick = jnp.where((row == column + shift) & (column < D_DEV), 1.0, 0.0).astype(BF16)
        part_b[n, 80:96] = jnp.dot(
            rest[:, first : first + 256], pick, preferred_element_type=F32
        ).astype(BF16)
    for copy in parts[1]:
        copy.start()

    txt.far()
    txt.got(7, 8, 9, 10)
    image_across.wait_recv()
    for n, (dy, _) in enumerate(ORDER):
        visit(image_far[...], chip(texts, dy), far_sum, n == 0)
    image_back_out[...] = far_sum[...].astype(BF16)
    image_back.start()
    for n, (dy, _) in enumerate(ORDER):
        if n:
            visit(images[own], chip(texts, dy), image_sum, False)

    def gathered(part, mine, count):
        total = mine[z].astype(F32)
        landed = (in_a, in_b)[part]
        for copy in parts[part]:
            copy.wait_recv()
        for n in range(7):
            total = total + landed[n].astype(F32)
        return total

    head_out[:, 0:128] = gathered(0, part_a, 80)[0:D_DEV]
    total = gathered(1, part_b, 96)
    head_out[:, 128:256] = total[0:D_DEV]
    tail = jnp.concatenate([total[80:96], jnp.zeros((112, 128), F32)], axis=0)
    head_out[:, 256:FF_DEV] = jnp.transpose(tail)[0:D_DEV, 0 : FF_DEV - 256]

    image_back.wait_recv()
    incoming = image_sum[...] + image_back_in[...].astype(F32)
    image_out[...] = unit_back(image_ref[...].astype(F32), incoming)

    img.finish()
    txt.finish()
    grd.finish()
    for copy in pieces + halves[1] + parts[0] + parts[1]:
        copy.wait_send()
    for copy in (image_across, text_across, text_back, image_back):
        copy.wait_send()


def local(image_emb, text_hidden, head_weight, positive, log_scale, bias):
    vmem = pl.BlockSpec(memory_space=pltpu.VMEM)
    dma = pltpu.SemaphoreType.DMA
    sends = len(SENDS)
    image_grad, head_turned = pl.pallas_call(
        kernel,
        out_shape=(
            jax.ShapeDtypeStruct((ROWS, D), F32),
            jax.ShapeDtypeStruct((D_DEV, FF_DEV), F32),
        ),
        in_specs=[vmem, vmem, pl.BlockSpec(memory_space=pl.ANY), vmem, vmem, vmem],
        out_specs=(vmem, vmem),
        scratch_shapes=[
            pltpu.VMEM((FF, D), BF16),
            pltpu.VMEM((8, ROWS, D), BF16),
            pltpu.VMEM((8, ROWS, D), BF16),
            pltpu.VMEM((8, ROWS, D), BF16),
            pltpu.VMEM((ROWS, D), BF16),
            pltpu.VMEM((ROWS, D), BF16),
            pltpu.VMEM((ROWS, D), F32),
            pltpu.VMEM((ROWS, D), F32),
            pltpu.VMEM((ROWS, D), F32),
            pltpu.VMEM((ROWS, D), F32),
            pltpu.VMEM((ROWS, D), BF16),
            pltpu.VMEM((ROWS, D), BF16),
            pltpu.VMEM((ROWS, D), BF16),
            pltpu.VMEM((ROWS, D), BF16),
            pltpu.VMEM((8, 2 * FF_PAD, ROWS), BF16),
            pltpu.VMEM((4, 2 * FF_PAD, 2 * ROWS), BF16),
            pltpu.VMEM((2 * FF_PAD, D), F32),
            pltpu.VMEM((2 * FF_PAD, D), BF16),
            pltpu.VMEM((3, FF_PAD, LANES), BF16),
            pltpu.VMEM((LANES, 128), F32),
            pltpu.VMEM((8, 80, 128), BF16),
            pltpu.VMEM((8, 96, 128), BF16),
            pltpu.VMEM((7, 80, 128), BF16),
            pltpu.VMEM((7, 96, 128), BF16),
            dma((9,)),
            dma((sends,)),
            dma((sends,)),
            dma((sends,)),
            dma((sends,)),
            dma((sends,)),
            dma((sends,)),
            dma((4,)),
            dma((4,)),
            dma((7,)),
            dma((7,)),
            dma((6,)),
            dma((6,)),
            dma((14,)),
            dma((14,)),
        ],
        compiler_params=pltpu.CompilerParams(
            collective_id=0, has_side_effects=True, vmem_limit_bytes=60 * 1024 * 1024
        ),
    )(
        image_emb,
        text_hidden.T,
        head_weight,
        positive,
        log_scale.reshape(1, 1),
        bias.reshape(1, 1),
    )
    return image_grad, head_turned.T


def solution(mesh):
    in_specs = (
        P(("grp", "blk"), None),
        P(("grp", "blk"), None),
        P(),
        P(("grp", "blk"), None),
        P(),
        P(),
    )
    out_specs = (P(("grp", "blk"), None), P("blk", "grp"))
    return jax.shard_map(local, mesh=mesh, in_specs=in_specs, out_specs=out_specs, check_vma=False)
```

```python
import jax
import jax.numpy as jnp
from jax import lax
from jax.experimental import pallas as pl
from jax.experimental.pallas import tpu as pltpu
from jax.sharding import PartitionSpec as P

MESH = pl.DeviceIdType.MESH
BF16 = jnp.bfloat16
F32 = jnp.float32

ROWS = 128
D = 1152
FF = 4304
FF_DEV = 269
FF_PAD = 272
WINDOW = 288
D_DEV = 72
LANES = 640
CHUNK = 512
A_ROWS, B_ROWS = 144, 128


def nt_dot(left, right):
    return lax.dot_general(left, right, (((1,), (1,)), ((), ())), preferred_element_type=F32)


def tn_dot(left, right):
    return lax.dot_general(left, right, (((0,), (0,)), ((), ())), preferred_element_type=F32)


class Place:
    def __init__(self):
        self.g = lax.axis_index("grp")
        self.b = lax.axis_index("blk")
        rest = lax.rem(self.b, 4)
        self.y, self.xh, self.c = lax.div(self.b, 4), lax.div(rest, 2), lax.rem(rest, 2)
        self.xl, self.z = lax.div(self.g, 8), lax.rem(self.g, 8)

    def slot(self, dy, flip_c):
        return self.turn(dy) * 2 + (1 - self.c if flip_c else self.c)

    def turn(self, dy):
        return lax.rem(self.y + dy, 4)

    def device(self, dy=0, flip_c=0, flip_xh=0, flip_xl=0, dz=0):
        c = 1 - self.c if flip_c else self.c
        xh = 1 - self.xh if flip_xh else self.xh
        xl = 1 - self.xl if flip_xl else self.xl
        return (xl * 8 + lax.rem(self.z + dz, 8), self.turn(dy) * 4 + xh * 2 + c)


FULL, LOW, HIGH = (0, ROWS), (0, ROWS // 2), (ROWS // 2, ROWS // 2)
OWN, UP, DOWN, FAR, TWIN = (0, 0), (1, 0), (3, 0), (2, 0), (0, 1)
SENDS = [
    (OWN, LOW, UP, DOWN),
    (OWN, HIGH, DOWN, UP),
    (OWN, HIGH, UP, DOWN),
    (OWN, LOW, DOWN, UP),
    (DOWN, LOW, UP, FAR),
    (UP, HIGH, DOWN, FAR),
    (OWN, FULL, TWIN, TWIN),
    (DOWN, FULL, TWIN, (3, 1)),
    (UP, FULL, TWIN, (1, 1)),
    (FAR, LOW, TWIN, (2, 1)),
    (FAR, HIGH, TWIN, (2, 1)),
]
ORDER = [(0, (6,)), (3, (7,)), (1, (8,)), (2, (9, 10))]


class Gather:
    def __init__(self, place, buf, send_sem, recv_sem):
        self.place, self.buf, self.send_sem, self.recv_sem = place, buf, send_sem, recv_sem
        self.held = []

    def copy(self, i, block):
        _, (first, count), target, _ = SENDS[i]
        ref = self.buf.at[self.place.slot(*block), pl.ds(first, count)]
        return pltpu.make_async_remote_copy(
            src_ref=ref,
            dst_ref=ref,
            send_sem=self.send_sem.at[i],
            recv_sem=self.recv_sem.at[i],
            device_id=self.place.device(*target),
            device_id_type=MESH,
        )

    def send(self, *which):
        for i in which:
            copy = self.copy(i, SENDS[i][0])
            copy.start()
            self.held.append(copy)

    def got(self, *which):
        for i in which:
            self.copy(i, SENDS[i][3]).wait_recv()

    def pass_on(self):
        self.got(0)
        self.send(4)
        self.got(1)
        self.send(5)

    def near(self):
        self.got(2)
        self.send(7)
        self.got(3)
        self.send(8)

    def far(self):
        self.got(4)
        self.send(9)
        self.got(5)
        self.send(10)

    def finish(self):
        for copy in self.held:
            copy.wait_send()


def kernel(
    image_ref, hidden_ref, weight_ref, positive_ref, scale_ref, bias_ref,
    image_out, head_out,
    weight_buf, images, texts, far_texts, grads, raw,
    text_sum, image_sum, far_sum, text_back_out, text_back_in,
    piece_out, piece_in, head, head_a, head_in, turned, turned_b,
    part_a, part_b, in_a, in_b, sum_b, far_b,
    weight_sem, img_send, img_recv, txt_send, txt_recv, far_send, far_recv, grd_send, grd_recv,
    x_send, x_recv, hid_send, hid_recv, half_send, half_recv, part_send, part_recv,
):
    place = Place()
    y, c, xh, xl, z = place.y, place.c, place.xh, place.xl, place.z
    own = place.slot(*OWN)

    barrier = pltpu.get_barrier_semaphore()
    peers = [place.device(dy, fc) for dy in range(4) for fc in range(2) if dy or fc]
    peers += [place.device(flip_xh=1), place.device(flip_xl=1), place.device(flip_xh=1, flip_xl=1)]
    peers += [place.device(dz=d) for d in range(1, 8)]
    for peer in peers:
        pl.semaphore_signal(barrier, inc=1, device_id=peer, device_id_type=MESH)

    bounds = [(k, min(CHUNK, FF - k)) for k in range(0, FF, CHUNK)]
    weight_copies = []
    for n, (first, count) in enumerate(bounds):
        rows = pl.ds(first, count)
        copy = pltpu.make_async_copy(weight_ref.at[rows], weight_buf.at[rows], weight_sem.at[n])
        copy.start()
        weight_copies.append(copy)

    def unit_of(values):
        norm = jnp.sqrt(jnp.sum(values * values, axis=-1, keepdims=True) + 1e-06)
        return norm, values / norm

    def unit_back(values, incoming):
        norm, direction = unit_of(values)
        along = jnp.sum(direction * incoming, axis=-1, keepdims=True)
        return (incoming - direction * along) / norm

    def remote(src, dst, send_sem, recv_sem, target):
        return pltpu.make_async_remote_copy(
            src_ref=src,
            dst_ref=dst,
            send_sem=send_sem,
            recv_sem=recv_sem,
            device_id=target,
            device_id_type=MESH,
        )

    img = Gather(place, images, img_send, img_recv)
    txt = Gather(place, texts, txt_send, txt_recv)
    far = Gather(place, far_texts, far_send, far_recv)
    grd = Gather(place, grads, grd_send, grd_recv)
    partner = place.device(flip_xh=1)
    text_across = remote(texts.at[own], far_texts.at[own], x_send.at[0], x_recv.at[0], partner)
    text_back = remote(text_back_out, text_back_in, x_send.at[1], x_recv.at[1], partner)

    def cut(start, first, window):
        row = lax.broadcasted_iota(jnp.int32, (FF_PAD, window), 0)
        column = lax.broadcasted_iota(jnp.int32, (FF_PAD, window), 1)
        wanted = jnp.where(row < 128, row, jnp.where(row < A_ROWS, row + 128, row - 16))
        pick = jnp.where(column == wanted + (start - first), 1.0, 0.0).astype(BF16)
        return jnp.dot(
            pick, hidden_ref[pl.ds(first, window)], preferred_element_type=F32
        ).astype(BF16)

    def cut_step(n, carry):
        start = n * FF_DEV
        first = pl.multiple_of(lax.div(start, 16) * 16, 16)
        column, half = lax.div(n, 4) * 2 + lax.rem(n, 2), lax.rem(lax.div(n, 2), 2)
        rows = pl.ds(pl.multiple_of(half * FF_PAD, 16), FF_PAD)
        piece_out[column, rows] = cut(start, first, WINDOW)
        return carry

    images[own] = unit_of(image_ref[...].astype(F32))[1].astype(BF16)
    lax.fori_loop(0, 5, cut_step, 0)
    pl.semaphore_wait(barrier, len(peers))
    img.send(0, 1, 2, 3, 6)
    lax.fori_loop(5, 15, cut_step, 0)
    last = 15 * FF_DEV
    piece_out[7, FF_PAD : 2 * FF_PAD] = cut(last, last // 16 * 16, FF - last // 16 * 16)

    for n, (first, count) in enumerate(bounds):
        weight_copies[n].wait()
        rows = pl.ds(first, count)
        term = tn_dot(hidden_ref[rows], weight_buf[rows])
        raw[...] = term if n == 0 else raw[...] + term
    texts[own] = unit_of(raw[...])[1].astype(BF16)
    text_across.start()
    txt.send(6)
    img.pass_on()

    def lane(core):
        return pl.ds(pl.multiple_of(core * ROWS, ROWS), ROWS)

    OTHERS = [(dy, fc) for dy in (1, 3, 2) for fc in range(2)] + [TWIN]

    def piece_copy(n, dy, fc, back=False):
        if back:
            dst = piece_in.at[place.turn(4 - dy), :, lane(1 - c if fc else c)]
        else:
            dst = piece_in.at[y, :, lane(c)]
        return remote(
            piece_out.at[place.slot(dy, fc)], dst, hid_send.at[n], hid_recv.at[n],
            place.device(dy, fc),
        )

    pieces = [piece_copy(n, *target) for n, target in enumerate(OTHERS)]
    for copy in pieces:
        copy.start()
    piece_in[y, :, lane(c)] = piece_out[own]
    img.near()

    logit_scale = jnp.exp(scale_ref[...])
    logit_bias = bias_ref[...]
    text_row = lax.broadcasted_iota(jnp.int32, (ROWS, ROWS), 0)
    label = jnp.where(text_row == positive_ref[...], 1.0, 0.0)

    def with_twin(value):
        return jnp.concatenate(
            [jnp.where(c == 0, value, 0.0), jnp.where(c == 0, 0.0, value)], axis=1
        )

    def chip(buf, dy):
        return buf[pl.ds(2 * place.turn(dy), 2)].reshape(2 * ROWS, D)

    def visit(unit, block, total, first, own_label=None):
        chance = jax.nn.sigmoid(logit_scale * nt_dot(unit, block) + logit_bias)
        if own_label is not None:
            chance = chance - with_twin(own_label)
        weight = (logit_scale * chance).astype(BF16)
        term = jnp.dot(weight, block, preferred_element_type=F32)
        total[...] = term if first else total[...] + term

    def visit_texts(n):
        label_of = label if n == 0 else None
        visit(texts[own], chip(images, ORDER[n][0]), text_sum, n == 0, label_of)

    def visit_far(n):
        visit(far_texts[own], chip(images, ORDER[n][0]), far_sum, n == 0)

    def visit_images(n, gather):
        own_label = jnp.transpose(label) if n == 0 and gather is txt else None
        block = chip(gather.buf, ORDER[n][0])
        visit(images[own], block, image_sum, own_label is not None, own_label)

    for n in range(3):
        img.got(*ORDER[n][1])
        visit_texts(n)
    img.far()
    txt.send(0, 1, 2, 3)
    text_across.wait_recv()
    far.send(6)
    for n in range(3):
        visit_far(n)
    img.got(*ORDER[3][1])
    visit_far(3)
    text_back_out[...] = far_sum[...].astype(BF16)
    text_back.start()
    visit_texts(3)
    text_back.wait_recv()
    incoming = text_sum[...] + text_back_in[...].astype(F32)
    grads[own] = unit_back(raw[...], incoming).astype(BF16)
    grd.send(0, 1, 6)
    txt.got(6)
    visit_images(0, txt)
    far.got(6)
    visit_images(0, far)
    grd.send(2, 3)
    for n, (dy, fc) in enumerate(OTHERS):
        piece_copy(n, dy, fc, back=True).wait_recv()

    def add_head(dy, n):
        term = jnp.dot(piece_in[place.turn(dy)], chip(grads, dy), preferred_element_type=F32)
        head[...] = term if n == 0 else head[...] + term

    grd.got(6)
    add_head(0, 0)
    grd.pass_on()
    grd.near()
    txt.pass_on()
    txt.near()
    grd.got(7)
    add_head(3, 1)
    grd.got(8)
    add_head(1, 2)
    grd.far()
    far.send(0, 1, 2, 3)
    grd.got(9, 10)
    add_head(2, 3)

    FLIPS = [(0, 1), (1, 0), (1, 1)]
    ROUND = (1, 7, 2, 6, 3, 5, 4)

    def window(half):
        return pl.ds(pl.multiple_of(half * 512, 128), LANES)

    def half_copy(n, flip_xh, flip_xl):
        to_xh = 1 - xh if flip_xh else xh
        to_xl = 1 - xl if flip_xl else xl
        return remote(
            head_a.at[to_xh, :, window(to_xl)], head_in.at[n], half_send.at[n], half_recv.at[n],
            place.device(flip_xh=flip_xh, flip_xl=flip_xl),
        )

    def late_copy(n, flip_xh, flip_xl):
        to_xh = 1 - xh if flip_xh else xh
        to_xl = 1 - xl if flip_xl else xl
        return remote(
            sum_b.at[2 * to_xh + to_xl], far_b.at[n], half_send.at[3 + n], half_recv.at[3 + n],
            place.device(flip_xh=flip_xh, flip_xl=flip_xl),
        )

    def part_copy(d, part):
        target = lax.rem(z + d, 8)
        src, dst = ((part_a, in_a), (part_b, in_b))[part]
        n = part * 7 + d - 1
        return remote(
            src.at[target], dst.at[d - 1], part_send.at[n], part_recv.at[n], place.device(dz=d)
        )

    halves = [half_copy(n, *flips) for n, flips in enumerate(FLIPS)]
    lates = [late_copy(n, *flips) for n, flips in enumerate(FLIPS)]
    parts = [[part_copy(d, part) for d in ROUND] for part in range(2)]

    for n in range(2):
        head_a[n] = head[n * FF_PAD : n * FF_PAD + A_ROWS].astype(BF16)
    for copy in halves:
        copy.start()
    for n in range(2):
        turned_b[...] = jnp.transpose(head[n * FF_PAD + A_ROWS : (n + 1) * FF_PAD])
        for half in range(2):
            for k in range(8):
                first = half * 8 * D_DEV + k * D_DEV
                part_b[k, 2 * n + half, 0:D_DEV] = turned_b[first : first + D_DEV].astype(BF16)
    for copy in parts[1]:
        copy.start()

    txt.far()
    for n in (1, 2):
        txt.got(*ORDER[n][1])
        visit_images(n, txt)
    far.pass_on()
    far.near()
    for n in (1, 2):
        far.got(*ORDER[n][1])
        visit_images(n, far)
    far.far()

    for copy in halves:
        copy.wait_recv()
    total = head[pl.ds(pl.multiple_of(xh * FF_PAD, 16), A_ROWS), window(xl)]
    for n in range(3):
        total = total + head_in[n].astype(F32)
    turned[...] = jnp.transpose(total[0:128])
    row = lax.broadcasted_iota(jnp.int32, (256, 128), 0)
    column = lax.broadcasted_iota(jnp.int32, (256, 128), 1)
    rest = total[128:A_ROWS].astype(BF16)
    for n in range(8):
        rows = pl.ds(pl.multiple_of(n * D_DEV + xl * 64, 8), D_DEV)
        part_a[n, 0:D_DEV] = turned[rows].astype(BF16)
        first = min(n * D_DEV // 128 * 128, LANES - 256)
        shift = n * D_DEV - first + 64 * xl
        pick = jnp.where((row == column + shift) & (column < D_DEV), 1.0, 0.0).astype(BF16)
        part_a[n, 80:96] = jnp.dot(
            rest[:, first : first + 256], pick, preferred_element_type=F32
        ).astype(BF16)
    for copy in parts[0]:
        copy.start()

    for gather in (txt, far):
        gather.got(*ORDER[3][1])
        visit_images(3, gather)
    image_out[...] = unit_back(image_ref[...].astype(F32), image_sum[...])

    for copy in parts[1]:
        copy.wait_recv()
    total = part_b[z].astype(F32)
    for n in range(7):
        total = total + in_b[n].astype(F32)
    sum_b[...] = total.astype(BF16)
    for copy in lates:
        copy.start()

    for copy in parts[0]:
        copy.wait_recv()
    total = part_a[z].astype(F32)
    for n in range(7):
        total = total + in_a[n].astype(F32)
    head_out[:, 0:128] = total[0:D_DEV]
    tail = jnp.concatenate([total[80:96], jnp.zeros((112, 128), F32)], axis=0)
    head_out[:, 256:FF_DEV] = jnp.transpose(tail)[0:D_DEV, 0 : FF_DEV - 256]
    for copy in lates:
        copy.wait_recv()
    total = sum_b[2 * xh + xl].astype(F32)
    for n in range(3):
        total = total + far_b[n].astype(F32)
    head_out[:, 128:256] = total[0:D_DEV]

    for gather in (img, txt, far, grd):
        gather.finish()
    for copy in pieces + halves + lates + parts[0] + parts[1] + [text_across, text_back]:
        copy.wait_send()


def settle(image_ref, head_ref, image_out, head_out):
    image_out[...] = image_ref[...]
    head_out[...] = head_ref[...]


def local(image_emb, text_hidden, head_weight, positive, log_scale, bias):
    vmem = pl.BlockSpec(memory_space=pltpu.VMEM)
    dma = pltpu.SemaphoreType.DMA
    sends = len(SENDS)
    image_grad, head_turned = pl.pallas_call(
        kernel,
        out_shape=(
            jax.ShapeDtypeStruct((ROWS, D), F32),
            jax.ShapeDtypeStruct((D_DEV, FF_DEV), F32),
        ),
        in_specs=[vmem, vmem, pl.BlockSpec(memory_space=pl.ANY), vmem, vmem, vmem],
        out_specs=(vmem, vmem),
        scratch_shapes=[
            pltpu.VMEM((FF, D), BF16),
            pltpu.VMEM((8, ROWS, D), BF16),
            pltpu.VMEM((8, ROWS, D), BF16),
            pltpu.VMEM((8, ROWS, D), BF16),
            pltpu.VMEM((8, ROWS, D), BF16),
            pltpu.VMEM((ROWS, D), F32),
            pltpu.VMEM((ROWS, D), F32),
            pltpu.VMEM((ROWS, D), F32),
            pltpu.VMEM((ROWS, D), F32),
            pltpu.VMEM((ROWS, D), BF16),
            pltpu.VMEM((ROWS, D), BF16),
            pltpu.VMEM((8, 2 * FF_PAD, ROWS), BF16),
            pltpu.VMEM((4, 2 * FF_PAD, 2 * ROWS), BF16),
            pltpu.VMEM((2 * FF_PAD, D), F32),
            pltpu.VMEM((2, A_ROWS, D), BF16),
            pltpu.VMEM((3, A_ROWS, LANES), BF16),
            pltpu.VMEM((LANES, 128), F32),
            pltpu.VMEM((D, 128), F32),
            pltpu.VMEM((8, 96, 128), BF16),
            pltpu.VMEM((8, 4, 80, 128), BF16),
            pltpu.VMEM((7, 96, 128), BF16),
            pltpu.VMEM((7, 4, 80, 128), BF16),
            pltpu.VMEM((4, 80, 128), BF16),
            pltpu.VMEM((3, 80, 128), BF16),
            dma((9,)),
            dma((sends,)),
            dma((sends,)),
            dma((sends,)),
            dma((sends,)),
            dma((sends,)),
            dma((sends,)),
            dma((sends,)),
            dma((sends,)),
            dma((2,)),
            dma((2,)),
            dma((7,)),
            dma((7,)),
            dma((6,)),
            dma((6,)),
            dma((14,)),
            dma((14,)),
        ],
        compiler_params=pltpu.CompilerParams(
            collective_id=0, has_side_effects=True, vmem_limit_bytes=60 * 1024 * 1024
        ),
    )(
        image_emb,
        text_hidden.T,
        head_weight,
        positive,
        log_scale.reshape(1, 1),
        bias.reshape(1, 1),
    )
    image_grad, head_turned = pl.pallas_call(
        settle,
        out_shape=(
            jax.ShapeDtypeStruct((ROWS, D), F32),
            jax.ShapeDtypeStruct((D_DEV, FF_DEV), F32),
        ),
        in_specs=[vmem, vmem],
        out_specs=(vmem, vmem),
        compiler_params=pltpu.CompilerParams(vmem_limit_bytes=60 * 1024 * 1024),
    )(image_grad, head_turned)
    return image_grad, head_turned.T


def solution(mesh):
    in_specs = (
        P(("grp", "blk"), None),
        P(("grp", "blk"), None),
        P(),
        P(("grp", "blk"), None),
        P(),
        P(),
    )
    out_specs = (P(("grp", "blk"), None), P("blk", "grp"))
    return jax.shard_map(local, mesh=mesh, in_specs=in_specs, out_specs=out_specs, check_vma=False)
```

```python
import jax
import jax.numpy as jnp
from jax import lax
from jax.experimental import pallas as pl
from jax.experimental.pallas import tpu as pltpu
from jax.sharding import PartitionSpec as P

MESH = pl.DeviceIdType.MESH
BF16 = jnp.bfloat16
F32 = jnp.float32

ROWS = 128
D = 1152
FF = 4304
FF_DEV = 269
FF_PAD = 272
WINDOW = 288
D_DEV = 72
LANES = 640
CHUNK = 512
A_ROWS, B_ROWS = 144, 128


def nt_dot(left, right):
    return lax.dot_general(left, right, (((1,), (1,)), ((), ())), preferred_element_type=F32)


def tn_dot(left, right):
    return lax.dot_general(left, right, (((0,), (0,)), ((), ())), preferred_element_type=F32)


class Place:
    def __init__(self):
        self.g = lax.axis_index("grp")
        self.b = lax.axis_index("blk")
        rest = lax.rem(self.b, 4)
        self.y, self.xh, self.c = lax.div(self.b, 4), lax.div(rest, 2), lax.rem(rest, 2)
        self.xl, self.z = lax.div(self.g, 8), lax.rem(self.g, 8)

    def slot(self, dy, flip_c):
        return self.turn(dy) * 2 + (1 - self.c if flip_c else self.c)

    def turn(self, dy):
        return lax.rem(self.y + dy, 4)

    def device(self, dy=0, flip_c=0, flip_xh=0, flip_xl=0, dz=0):
        c = 1 - self.c if flip_c else self.c
        xh = 1 - self.xh if flip_xh else self.xh
        xl = 1 - self.xl if flip_xl else self.xl
        return (xl * 8 + lax.rem(self.z + dz, 8), self.turn(dy) * 4 + xh * 2 + c)


FULL, LOW, HIGH = (0, ROWS), (0, ROWS // 2), (ROWS // 2, ROWS // 2)
OWN, UP, DOWN, FAR, TWIN = (0, 0), (1, 0), (3, 0), (2, 0), (0, 1)
SENDS = [
    (OWN, LOW, UP, DOWN),
    (OWN, HIGH, DOWN, UP),
    (OWN, HIGH, UP, DOWN),
    (OWN, LOW, DOWN, UP),
    (DOWN, LOW, UP, FAR),
    (UP, HIGH, DOWN, FAR),
    (OWN, FULL, TWIN, TWIN),
    (DOWN, FULL, TWIN, (3, 1)),
    (UP, FULL, TWIN, (1, 1)),
    (FAR, LOW, TWIN, (2, 1)),
    (FAR, HIGH, TWIN, (2, 1)),
]
ORDER = [(0, (6,)), (3, (7,)), (1, (8,)), (2, (9, 10))]


class Gather:
    def __init__(self, place, buf, send_sem, recv_sem):
        self.place, self.buf, self.send_sem, self.recv_sem = place, buf, send_sem, recv_sem
        self.held = []

    def copy(self, i, block):
        _, (first, count), target, _ = SENDS[i]
        ref = self.buf.at[self.place.slot(*block), pl.ds(first, count)]
        return pltpu.make_async_remote_copy(
            src_ref=ref,
            dst_ref=ref,
            send_sem=self.send_sem.at[i],
            recv_sem=self.recv_sem.at[i],
            device_id=self.place.device(*target),
            device_id_type=MESH,
        )

    def send(self, *which):
        for i in which:
            copy = self.copy(i, SENDS[i][0])
            copy.start()
            self.held.append(copy)

    def got(self, *which):
        for i in which:
            self.copy(i, SENDS[i][3]).wait_recv()

    def pass_on(self):
        self.got(0)
        self.send(4)
        self.got(1)
        self.send(5)

    def near(self):
        self.got(2)
        self.send(7)
        self.got(3)
        self.send(8)

    def far(self):
        self.got(4)
        self.send(9)
        self.got(5)
        self.send(10)

    def finish(self):
        for copy in self.held:
            copy.wait_send()


def kernel(
    image_ref, hidden_ref, weight_ref, positive_ref, scale_ref, bias_ref,
    image_out, head_out,
    weight_buf, images, texts, far_texts, grads, raw,
    text_sum, image_sum, far_sum, text_back_out, text_back_in,
    piece_out, piece_in, head, head_a, head_in, turned, turned_b,
    part_a, part_b, in_a, in_b, sum_b, far_b,
    weight_sem, img_send, img_recv, txt_send, txt_recv, far_send, far_recv, grd_send, grd_recv,
    x_send, x_recv, hid_send, hid_recv, half_send, half_recv, part_send, part_recv,
):
    place = Place()
    y, c, xh, xl, z = place.y, place.c, place.xh, place.xl, place.z
    own = place.slot(*OWN)

    barrier = pltpu.get_barrier_semaphore()
    peers = [place.device(dy, fc) for dy in range(4) for fc in range(2) if dy or fc]
    peers += [place.device(flip_xh=1), place.device(flip_xl=1), place.device(flip_xh=1, flip_xl=1)]
    peers += [place.device(dz=d) for d in range(1, 8)]
    for peer in peers:
        pl.semaphore_signal(barrier, inc=1, device_id=peer, device_id_type=MESH)

    bounds = [(k, min(CHUNK, FF - k)) for k in range(0, FF, CHUNK)]
    weight_copies = []
    for n, (first, count) in enumerate(bounds):
        rows = pl.ds(first, count)
        copy = pltpu.make_async_copy(weight_ref.at[rows], weight_buf.at[rows], weight_sem.at[n])
        copy.start()
        weight_copies.append(copy)

    def unit_of(values):
        norm = jnp.sqrt(jnp.sum(values * values, axis=-1, keepdims=True) + 1e-06)
        return norm, values / norm

    def unit_back(values, incoming):
        norm, direction = unit_of(values)
        along = jnp.sum(direction * incoming, axis=-1, keepdims=True)
        return (incoming - direction * along) / norm

    def remote(src, dst, send_sem, recv_sem, target):
        return pltpu.make_async_remote_copy(
            src_ref=src,
            dst_ref=dst,
            send_sem=send_sem,
            recv_sem=recv_sem,
            device_id=target,
            device_id_type=MESH,
        )

    img = Gather(place, images, img_send, img_recv)
    txt = Gather(place, texts, txt_send, txt_recv)
    far = Gather(place, far_texts, far_send, far_recv)
    grd = Gather(place, grads, grd_send, grd_recv)
    partner = place.device(flip_xh=1)
    text_across = remote(texts.at[own], far_texts.at[own], x_send.at[0], x_recv.at[0], partner)
    text_back = remote(text_back_out, text_back_in, x_send.at[1], x_recv.at[1], partner)

    def cut(start, first, window):
        row = lax.broadcasted_iota(jnp.int32, (FF_PAD, window), 0)
        column = lax.broadcasted_iota(jnp.int32, (FF_PAD, window), 1)
        wanted = jnp.where(row < 128, row, jnp.where(row < A_ROWS, row + 128, row - 16))
        pick = jnp.where(column == wanted + (start - first), 1.0, 0.0).astype(BF16)
        return jnp.dot(
            pick, hidden_ref[pl.ds(first, window)], preferred_element_type=F32
        ).astype(BF16)

    def cut_step(n, carry):
        start = n * FF_DEV
        first = pl.multiple_of(lax.div(start, 16) * 16, 16)
        column, half = lax.div(n, 4) * 2 + lax.rem(n, 2), lax.rem(lax.div(n, 2), 2)
        rows = pl.ds(pl.multiple_of(half * FF_PAD, 16), FF_PAD)
        piece_out[column, rows] = cut(start, first, WINDOW)
        return carry

    images[own] = unit_of(image_ref[...].astype(F32))[1].astype(BF16)
    lax.fori_loop(0, 5, cut_step, 0)
    pl.semaphore_wait(barrier, len(peers))
    img.send(0, 1, 2, 3, 6)
    lax.fori_loop(5, 15, cut_step, 0)
    last = 15 * FF_DEV
    piece_out[7, FF_PAD : 2 * FF_PAD] = cut(last, last // 16 * 16, FF - last // 16 * 16)

    for n, (first, count) in enumerate(bounds):
        weight_copies[n].wait()
        rows = pl.ds(first, count)
        term = tn_dot(hidden_ref[rows], weight_buf[rows])
        raw[...] = term if n == 0 else raw[...] + term
    texts[own] = unit_of(raw[...])[1].astype(BF16)
    text_across.start()
    txt.send(6)
    img.pass_on()

    def lane(core):
        return pl.ds(pl.multiple_of(core * ROWS, ROWS), ROWS)

    OTHERS = [(dy, fc) for dy in (1, 3, 2) for fc in range(2)] + [TWIN]

    def piece_copy(n, dy, fc, back=False):
        if back:
            dst = piece_in.at[place.turn(4 - dy), :, lane(1 - c if fc else c)]
        else:
            dst = piece_in.at[y, :, lane(c)]
        return remote(
            piece_out.at[place.slot(dy, fc)], dst, hid_send.at[n], hid_recv.at[n],
            place.device(dy, fc),
        )

    pieces = [piece_copy(n, *target) for n, target in enumerate(OTHERS)]
    piece_in[y, :, lane(c)] = piece_out[own]
    img.near()

    logit_scale = jnp.exp(scale_ref[...])
    logit_bias = bias_ref[...]
    text_row = lax.broadcasted_iota(jnp.int32, (ROWS, ROWS), 0)
    label = jnp.where(text_row == positive_ref[...], 1.0, 0.0)

    def with_twin(value):
        return jnp.concatenate(
            [jnp.where(c == 0, value, 0.0), jnp.where(c == 0, 0.0, value)], axis=1
        )

    def chip(buf, dy):
        return buf[pl.ds(2 * place.turn(dy), 2)].reshape(2 * ROWS, D)

    def visit(unit, block, total, first, own_label=None):
        chance = jax.nn.sigmoid(logit_scale * nt_dot(unit, block) + logit_bias)
        if own_label is not None:
            chance = chance - with_twin(own_label)
        weight = (logit_scale * chance).astype(BF16)
        term = jnp.dot(weight, block, preferred_element_type=F32)
        total[...] = term if first else total[...] + term

    def visit_texts(n):
        label_of = label if n == 0 else None
        visit(texts[own], chip(images, ORDER[n][0]), text_sum, n == 0, label_of)

    def visit_far(n):
        visit(far_texts[own], chip(images, ORDER[n][0]), far_sum, n == 0)

    def visit_images(n, gather):
        own_label = jnp.transpose(label) if n == 0 and gather is txt else None
        block = chip(gather.buf, ORDER[n][0])
        visit(images[own], block, image_sum, own_label is not None, own_label)

    for n in range(3):
        img.got(*ORDER[n][1])
        visit_texts(n)
    img.far()
    for copy in pieces:
        copy.start()
    text_across.wait_recv()
    far.send(6)
    for n in range(3):
        visit_far(n)
    img.got(*ORDER[3][1])
    visit_far(3)
    text_back_out[...] = far_sum[...].astype(BF16)
    text_back.start()
    visit_texts(3)
    text_back.wait_recv()
    incoming = text_sum[...] + text_back_in[...].astype(F32)
    grads[own] = unit_back(raw[...], incoming).astype(BF16)
    grd.send(0, 1, 6)
    txt.got(6)
    visit_images(0, txt)
    far.got(6)
    visit_images(0, far)
    grd.send(2, 3)
    for n, (dy, fc) in enumerate(OTHERS):
        piece_copy(n, dy, fc, back=True).wait_recv()

    def add_head(dy, n):
        term = jnp.dot(piece_in[place.turn(dy)], chip(grads, dy), preferred_element_type=F32)
        head[...] = term if n == 0 else head[...] + term

    grd.got(6)
    add_head(0, 0)
    grd.pass_on()
    grd.near()
    grd.got(7)
    add_head(3, 1)
    grd.got(8)
    add_head(1, 2)
    grd.far()
    txt.send(0, 1, 2, 3)
    grd.got(9, 10)
    last_piece, last_grads = piece_in.at[place.turn(2)], chip(grads, 2)

    def add_last(rows):
        term = jnp.dot(last_piece[rows], last_grads, preferred_element_type=F32)
        return head[rows] + term

    FLIPS = [(0, 1), (1, 0), (1, 1)]
    ROUND = (1, 7, 2, 6, 3, 5, 4)

    def window(half):
        return pl.ds(pl.multiple_of(half * 512, 128), LANES)

    def half_copy(n, flip_xh, flip_xl):
        to_xh = 1 - xh if flip_xh else xh
        to_xl = 1 - xl if flip_xl else xl
        return remote(
            head_a.at[to_xh, :, window(to_xl)], head_in.at[n], half_send.at[n], half_recv.at[n],
            place.device(flip_xh=flip_xh, flip_xl=flip_xl),
        )

    def late_copy(n, flip_xh, flip_xl):
        to_xh = 1 - xh if flip_xh else xh
        to_xl = 1 - xl if flip_xl else xl
        return remote(
            sum_b.at[2 * to_xh + to_xl], far_b.at[n], half_send.at[3 + n], half_recv.at[3 + n],
            place.device(flip_xh=flip_xh, flip_xl=flip_xl),
        )

    def part_copy(d, part):
        target = lax.rem(z + d, 8)
        src, dst = ((part_a, in_a), (part_b, in_b))[part]
        n = part * 7 + d - 1
        return remote(
            src.at[target], dst.at[d - 1], part_send.at[n], part_recv.at[n], place.device(dz=d)
        )

    halves = [half_copy(n, *flips) for n, flips in enumerate(FLIPS)]
    lates = [late_copy(n, *flips) for n, flips in enumerate(FLIPS)]
    parts = [[part_copy(d, part) for d in ROUND] for part in range(2)]

    for n in range(2):
        rows = pl.ds(n * FF_PAD + A_ROWS, B_ROWS)
        turned_b[...] = jnp.transpose(add_last(rows))
        for half in range(2):
            for k in range(8):
                first = half * 8 * D_DEV + k * D_DEV
                part_b[k, 2 * n + half, 0:D_DEV] = turned_b[first : first + D_DEV].astype(BF16)
    for copy in parts[1]:
        copy.start()
    for n in range(2):
        rows = pl.ds(n * FF_PAD, A_ROWS)
        total = add_last(rows)
        head[rows] = total
        head_a[n] = total.astype(BF16)
    for copy in halves:
        copy.start()

    far.send(0, 1, 2, 3)
    txt.pass_on()
    txt.near()
    for n in (1, 2):
        txt.got(*ORDER[n][1])
        visit_images(n, txt)

    for copy in halves:
        copy.wait_recv()
    total = head[pl.ds(pl.multiple_of(xh * FF_PAD, 16), A_ROWS), window(xl)]
    for n in range(3):
        total = total + head_in[n].astype(F32)
    turned[...] = jnp.transpose(total[0:128])
    row = lax.broadcasted_iota(jnp.int32, (256, 128), 0)
    column = lax.broadcasted_iota(jnp.int32, (256, 128), 1)
    rest = total[128:A_ROWS].astype(BF16)
    for n in range(8):
        rows = pl.ds(pl.multiple_of(n * D_DEV + xl * 64, 8), D_DEV)
        part_a[n, 0:D_DEV] = turned[rows].astype(BF16)
        first = min(n * D_DEV // 128 * 128, LANES - 256)
        shift = n * D_DEV - first + 64 * xl
        pick = jnp.where((row == column + shift) & (column < D_DEV), 1.0, 0.0).astype(BF16)
        part_a[n, 80:96] = jnp.dot(
            rest[:, first : first + 256], pick, preferred_element_type=F32
        ).astype(BF16)
    for copy in parts[0]:
        copy.start()

    far.pass_on()
    txt.far()
    far.near()
    txt.got(*ORDER[3][1])
    visit_images(3, txt)

    for copy in parts[1]:
        copy.wait_recv()
    total = part_b[z].astype(F32)
    for n in range(7):
        total = total + in_b[n].astype(F32)
    sum_b[...] = total.astype(BF16)
    for copy in lates:
        copy.start()

    for n in (1, 2):
        far.got(*ORDER[n][1])
        visit_images(n, far)
    far.far()
    far.got(*ORDER[3][1])
    visit_images(3, far)
    image_out[...] = unit_back(image_ref[...].astype(F32), image_sum[...])

    for copy in parts[0]:
        copy.wait_recv()
    total = part_a[z].astype(F32)
    for n in range(7):
        total = total + in_a[n].astype(F32)
    head_out[:, 0:128] = total[0:D_DEV]
    tail = jnp.concatenate([total[80:96], jnp.zeros((112, 128), F32)], axis=0)
    head_out[:, 256:FF_DEV] = jnp.transpose(tail)[0:D_DEV, 0 : FF_DEV - 256]
    for copy in lates:
        copy.wait_recv()
    total = sum_b[2 * xh + xl].astype(F32)
    for n in range(3):
        total = total + far_b[n].astype(F32)
    head_out[:, 128:256] = total[0:D_DEV]

    for gather in (img, txt, far, grd):
        gather.finish()
    for copy in pieces + halves + lates + parts[0] + parts[1] + [text_across, text_back]:
        copy.wait_send()


def settle(image_ref, head_ref, image_out, head_out):
    image_out[...] = image_ref[...]
    head_out[...] = head_ref[...]


def local(image_emb, text_hidden, head_weight, positive, log_scale, bias):
    vmem = pl.BlockSpec(memory_space=pltpu.VMEM)
    dma = pltpu.SemaphoreType.DMA
    sends = len(SENDS)
    image_grad, head_turned = pl.pallas_call(
        kernel,
        out_shape=(
            jax.ShapeDtypeStruct((ROWS, D), F32),
            jax.ShapeDtypeStruct((D_DEV, FF_DEV), F32),
        ),
        in_specs=[vmem, vmem, pl.BlockSpec(memory_space=pl.ANY), vmem, vmem, vmem],
        out_specs=(vmem, vmem),
        scratch_shapes=[
            pltpu.VMEM((FF, D), BF16),
            pltpu.VMEM((8, ROWS, D), BF16),
            pltpu.VMEM((8, ROWS, D), BF16),
            pltpu.VMEM((8, ROWS, D), BF16),
            pltpu.VMEM((8, ROWS, D), BF16),
            pltpu.VMEM((ROWS, D), F32),
            pltpu.VMEM((ROWS, D), F32),
            pltpu.VMEM((ROWS, D), F32),
            pltpu.VMEM((ROWS, D), F32),
            pltpu.VMEM((ROWS, D), BF16),
            pltpu.VMEM((ROWS, D), BF16),
            pltpu.VMEM((8, 2 * FF_PAD, ROWS), BF16),
            pltpu.VMEM((4, 2 * FF_PAD, 2 * ROWS), BF16),
            pltpu.VMEM((2 * FF_PAD, D), F32),
            pltpu.VMEM((2, A_ROWS, D), BF16),
            pltpu.VMEM((3, A_ROWS, LANES), BF16),
            pltpu.VMEM((LANES, 128), F32),
            pltpu.VMEM((D, 128), F32),
            pltpu.VMEM((8, 96, 128), BF16),
            pltpu.VMEM((8, 4, 80, 128), BF16),
            pltpu.VMEM((7, 96, 128), BF16),
            pltpu.VMEM((7, 4, 80, 128), BF16),
            pltpu.VMEM((4, 80, 128), BF16),
            pltpu.VMEM((3, 80, 128), BF16),
            dma((9,)),
            dma((sends,)),
            dma((sends,)),
            dma((sends,)),
            dma((sends,)),
            dma((sends,)),
            dma((sends,)),
            dma((sends,)),
            dma((sends,)),
            dma((2,)),
            dma((2,)),
            dma((7,)),
            dma((7,)),
            dma((6,)),
            dma((6,)),
            dma((14,)),
            dma((14,)),
        ],
        compiler_params=pltpu.CompilerParams(
            collective_id=0, has_side_effects=True, vmem_limit_bytes=60 * 1024 * 1024
        ),
    )(
        image_emb,
        text_hidden.T,
        head_weight,
        positive,
        log_scale.reshape(1, 1),
        bias.reshape(1, 1),
    )
    image_grad, head_turned = pl.pallas_call(
        settle,
        out_shape=(
            jax.ShapeDtypeStruct((ROWS, D), F32),
            jax.ShapeDtypeStruct((D_DEV, FF_DEV), F32),
        ),
        in_specs=[vmem, vmem],
        out_specs=(vmem, vmem),
        compiler_params=pltpu.CompilerParams(vmem_limit_bytes=60 * 1024 * 1024),
    )(image_grad, head_turned)
    return image_grad, head_turned.T


def solution(mesh):
    in_specs = (
        P(("grp", "blk"), None),
        P(("grp", "blk"), None),
        P(),
        P(("grp", "blk"), None),
        P(),
        P(),
    )
    out_specs = (P(("grp", "blk"), None), P("blk", "grp"))
    return jax.shard_map(local, mesh=mesh, in_specs=in_specs, out_specs=out_specs, check_vma=False)
```

```python
import jax
import jax.numpy as jnp
from jax import lax
from jax.experimental import pallas as pl
from jax.experimental.pallas import tpu as pltpu
from jax.sharding import PartitionSpec as P

MESH = pl.DeviceIdType.MESH
BF16 = jnp.bfloat16
F32 = jnp.float32

ROWS = 128
D = 1152
FF = 4304
FF_DEV = 269
FF_PAD = 272
WINDOW = 288
D_DEV = 72
LANES = 640
CHUNK = 512
A_ROWS, B_ROWS = 144, 128
LOW_LANES, HIGH_LANES = (0, LANES), (LANES, D - LANES)


def nt_dot(left, right):
    return lax.dot_general(left, right, (((1,), (1,)), ((), ())), preferred_element_type=F32)


def tn_dot(left, right):
    return lax.dot_general(left, right, (((0,), (0,)), ((), ())), preferred_element_type=F32)


class Place:
    def __init__(self):
        self.g = lax.axis_index("grp")
        self.b = lax.axis_index("blk")
        rest = lax.rem(self.b, 4)
        self.y, self.xh, self.c = lax.div(self.b, 4), lax.div(rest, 2), lax.rem(rest, 2)
        self.xl, self.z = lax.div(self.g, 8), lax.rem(self.g, 8)

    def slot(self, dy, flip_c):
        return self.turn(dy) * 2 + (1 - self.c if flip_c else self.c)

    def turn(self, dy):
        return lax.rem(self.y + dy, 4)

    def device(self, dy=0, flip_c=0, flip_xh=0, flip_xl=0, dz=0):
        c = 1 - self.c if flip_c else self.c
        xh = 1 - self.xh if flip_xh else self.xh
        xl = 1 - self.xl if flip_xl else self.xl
        return (xl * 8 + lax.rem(self.z + dz, 8), self.turn(dy) * 4 + xh * 2 + c)


FULL, LOW, HIGH = (0, ROWS), (0, ROWS // 2), (ROWS // 2, ROWS // 2)
OWN, UP, DOWN, FAR, TWIN = (0, 0), (1, 0), (3, 0), (2, 0), (0, 1)
SENDS = [
    (OWN, LOW, UP, DOWN),
    (OWN, HIGH, DOWN, UP),
    (OWN, HIGH, UP, DOWN),
    (OWN, LOW, DOWN, UP),
    (DOWN, LOW, UP, FAR),
    (UP, HIGH, DOWN, FAR),
    (OWN, FULL, TWIN, TWIN),
    (DOWN, FULL, TWIN, (3, 1)),
    (UP, FULL, TWIN, (1, 1)),
    (FAR, LOW, TWIN, (2, 1)),
    (FAR, HIGH, TWIN, (2, 1)),
]
ORDER = [(0, (6,)), (3, (7,)), (1, (8,)), (2, (9, 10))]


class Gather:
    def __init__(self, place, buf, send_sem, recv_sem, lanes=(0, D)):
        self.place, self.buf, self.send_sem, self.recv_sem = place, buf, send_sem, recv_sem
        self.lanes = pl.ds(*lanes)
        self.held = []

    def copy(self, i, block):
        _, (first, count), target, _ = SENDS[i]
        ref = self.buf.at[self.place.slot(*block), pl.ds(first, count), self.lanes]
        return pltpu.make_async_remote_copy(
            src_ref=ref,
            dst_ref=ref,
            send_sem=self.send_sem.at[i],
            recv_sem=self.recv_sem.at[i],
            device_id=self.place.device(*target),
            device_id_type=MESH,
        )

    def send(self, *which):
        for i in which:
            copy = self.copy(i, SENDS[i][0])
            copy.start()
            self.held.append(copy)

    def got(self, *which):
        for i in which:
            self.copy(i, SENDS[i][3]).wait_recv()

    def pass_on(self):
        self.got(0)
        self.send(4)
        self.got(1)
        self.send(5)

    def near(self):
        self.got(2)
        self.send(7)
        self.got(3)
        self.send(8)

    def far(self):
        self.got(4)
        self.send(9)
        self.got(5)
        self.send(10)

    def finish(self):
        for copy in self.held:
            copy.wait_send()


def kernel(
    image_ref, hidden_ref, weight_ref, positive_ref, scale_ref, bias_ref,
    image_out, head_out,
    weight_buf, images, texts, far_texts, grads, raw, text_sum, image_sum, far_sum,
    text_back_out, text_back_in,
    piece_out, piece_in, head, head_a, head_in, turned, turned_b,
    part_a, part_b, in_a, in_b, sum_b, far_b,
    weight_sem, img_send, img_recv, txt_send, txt_recv, far_send, far_recv,
    low_send, low_recv, high_send, high_recv,
    x_send, x_recv, hid_send, hid_recv, half_send, half_recv, part_send, part_recv,
):
    place = Place()
    y, c, xh, xl, z = place.y, place.c, place.xh, place.xl, place.z
    own = place.slot(*OWN)

    barrier = pltpu.get_barrier_semaphore()
    peers = [place.device(dy, fc) for dy in range(4) for fc in range(2) if dy or fc]
    peers += [place.device(flip_xh=1), place.device(flip_xl=1), place.device(flip_xh=1, flip_xl=1)]
    peers += [place.device(dz=d) for d in range(1, 8)]
    for peer in peers:
        pl.semaphore_signal(barrier, inc=1, device_id=peer, device_id_type=MESH)

    bounds = [(k, min(CHUNK, FF - k)) for k in range(0, FF, CHUNK)]
    weight_copies = []
    for n, (first, count) in enumerate(bounds):
        rows = pl.ds(first, count)
        copy = pltpu.make_async_copy(weight_ref.at[rows], weight_buf.at[rows], weight_sem.at[n])
        copy.start()
        weight_copies.append(copy)

    def unit_of(values):
        norm = jnp.sqrt(jnp.sum(values * values, axis=-1, keepdims=True) + 1e-06)
        return norm, values / norm

    def unit_back(values, incoming):
        norm, direction = unit_of(values)
        along = jnp.sum(direction * incoming, axis=-1, keepdims=True)
        return (incoming - direction * along) / norm

    def remote(src, dst, send_sem, recv_sem, target):
        return pltpu.make_async_remote_copy(
            src_ref=src,
            dst_ref=dst,
            send_sem=send_sem,
            recv_sem=recv_sem,
            device_id=target,
            device_id_type=MESH,
        )

    img = Gather(place, images, img_send, img_recv)
    txt = Gather(place, texts, txt_send, txt_recv)
    far = Gather(place, far_texts, far_send, far_recv)
    grds = [
        Gather(place, grads, low_send, low_recv, LOW_LANES),
        Gather(place, grads, high_send, high_recv, HIGH_LANES),
    ]
    partner = place.device(flip_xh=1)

    def across(n, src, dst):
        return remote(src, dst, x_send.at[n], x_recv.at[n], partner)

    text_across = across(0, texts.at[own], far_texts.at[own])
    text_back = across(1, text_back_out, text_back_in)

    def cut(start, first, window):
        row = lax.broadcasted_iota(jnp.int32, (FF_PAD, window), 0)
        column = lax.broadcasted_iota(jnp.int32, (FF_PAD, window), 1)
        wanted = jnp.where(row < 128, row, jnp.where(row < A_ROWS, row + 128, row - 16))
        pick = jnp.where(column == wanted + (start - first), 1.0, 0.0).astype(BF16)
        return jnp.dot(
            pick, hidden_ref[pl.ds(first, window)], preferred_element_type=F32
        ).astype(BF16)

    def cut_step(n, carry):
        start = n * FF_DEV
        first = pl.multiple_of(lax.div(start, 16) * 16, 16)
        column, half = lax.div(n, 4) * 2 + lax.rem(n, 2), lax.rem(lax.div(n, 2), 2)
        rows = pl.ds(pl.multiple_of(half * FF_PAD, 16), FF_PAD)
        piece_out[column, rows] = cut(start, first, WINDOW)
        return carry

    images[own] = unit_of(image_ref[...].astype(F32))[1].astype(BF16)
    lax.fori_loop(0, 5, cut_step, 0)
    pl.semaphore_wait(barrier, len(peers))
    img.send(0, 1, 6)
    lax.fori_loop(5, 11, cut_step, 0)
    img.send(2, 3)
    lax.fori_loop(11, 15, cut_step, 0)
    last = 15 * FF_DEV
    piece_out[7, FF_PAD : 2 * FF_PAD] = cut(last, last // 16 * 16, FF - last // 16 * 16)

    for n, (first, count) in enumerate(bounds):
        weight_copies[n].wait()
        rows = pl.ds(first, count)
        term = tn_dot(hidden_ref[rows], weight_buf[rows])
        raw[...] = term if n == 0 else raw[...] + term
    texts[own] = unit_of(raw[...])[1].astype(BF16)
    text_across.start()
    txt.send(6)
    img.pass_on()

    def lane(core):
        return pl.ds(pl.multiple_of(core * ROWS, ROWS), ROWS)

    OTHERS = [(dy, fc) for dy in (1, 3, 2) for fc in range(2)] + [TWIN]

    def piece_copy(n, dy, fc, back=False):
        if back:
            dst = piece_in.at[place.turn(4 - dy), :, lane(1 - c if fc else c)]
        else:
            dst = piece_in.at[y, :, lane(c)]
        return remote(
            piece_out.at[place.slot(dy, fc)], dst, hid_send.at[n], hid_recv.at[n],
            place.device(dy, fc),
        )

    pieces = [piece_copy(n, *target) for n, target in enumerate(OTHERS)]
    piece_in[y, :, lane(c)] = piece_out[own]
    img.near()
    for copy in pieces:
        copy.start()

    logit_scale = jnp.exp(jnp.full((1, 2 * ROWS), scale_ref[0], F32))
    logit_bias = bias_ref[0]
    text_row = lax.broadcasted_iota(jnp.int32, (ROWS, ROWS), 0)
    label = jnp.where(text_row == positive_ref[...], 1.0, 0.0)

    def with_twin(value):
        return jnp.concatenate(
            [jnp.where(c == 0, value, 0.0), jnp.where(c == 0, 0.0, value)], axis=1
        )

    def chip(buf, dy):
        return buf[pl.ds(2 * place.turn(dy), 2)].reshape(2 * ROWS, D)

    def visit(unit, block, total, first, own_label=None):
        chance = jax.nn.sigmoid(logit_scale * nt_dot(unit, block) + logit_bias)
        if own_label is not None:
            chance = chance - with_twin(own_label)
        weight = (logit_scale * chance).astype(BF16)
        term = jnp.dot(weight, block, preferred_element_type=F32)
        total[...] = term if first else total[...] + term

    def visit_texts(n):
        label_of = label if n == 0 else None
        visit(texts[own], chip(images, ORDER[n][0]), text_sum, n == 0, label_of)

    def visit_far_texts(n):
        visit(far_texts[own], chip(images, ORDER[n][0]), far_sum, n == 0)

    def visit_images(n, gather):
        gather.got(*ORDER[n][1])
        own_label = jnp.transpose(label) if n == 0 and gather is txt else None
        block = chip(gather.buf, ORDER[n][0])
        visit(images[own], block, image_sum, own_label is not None, own_label)

    for n in range(3):
        img.got(*ORDER[n][1])
        visit_texts(n)
    img.far()
    txt.send(0, 1, 2, 3)
    text_across.wait_recv()
    far.send(6)
    for n in range(3):
        visit_far_texts(n)
    img.got(*ORDER[3][1])
    visit_far_texts(3)
    text_back_out[...] = far_sum[...].astype(BF16)
    text_back.start()
    visit_texts(3)
    visit_images(0, txt)
    visit_images(0, far)
    text_back.wait_recv()
    incoming = text_sum[...] + text_back_in[...].astype(F32)
    grads[own] = unit_back(raw[...], incoming).astype(BF16)
    grds[0].send(0, 1, 2, 3, 6)
    for n, (dy, fc) in enumerate(OTHERS):
        piece_copy(n, dy, fc, back=True).wait_recv()

    def head_term(part, n, rows):
        first, count = (LOW_LANES, HIGH_LANES)[part]
        lanes = pl.ds(first, count)
        turn = place.turn(ORDER[n][0])
        block = grads[pl.ds(2 * turn, 2), :, lanes].reshape(2 * ROWS, count)
        term = jnp.dot(piece_in[turn, rows], block, preferred_element_type=F32)
        return term if n == 0 else head[rows, lanes] + term

    def add_head(part, n):
        grds[part].got(*ORDER[n][1])
        head[:, pl.ds(*(LOW_LANES, HIGH_LANES)[part])] = head_term(part, n, pl.ds(0, 2 * FF_PAD))

    add_head(0, 0)
    grds[0].pass_on()
    grds[1].send(0, 1, 2, 3, 6)
    grds[0].near()
    add_head(0, 1)
    add_head(0, 2)
    grds[0].far()
    grds[1].pass_on()

    FLIPS = [(0, 1), (1, 0), (1, 1)]
    ROUND = (1, 7, 2, 6, 3, 5, 4)

    def window(half):
        return pl.ds(pl.multiple_of(half * 512, 128), LANES)

    def half_copy(n, flip_xh, flip_xl):
        to_xh = 1 - xh if flip_xh else xh
        to_xl = 1 - xl if flip_xl else xl
        return remote(
            head_a.at[to_xh, :, window(to_xl)], head_in.at[n], half_send.at[n], half_recv.at[n],
            place.device(flip_xh=flip_xh, flip_xl=flip_xl),
        )

    def late_copy(n, flip_xh, flip_xl):
        to_xh = 1 - xh if flip_xh else xh
        to_xl = 1 - xl if flip_xl else xl
        return remote(
            sum_b.at[2 * to_xl + to_xh], far_b.at[n], half_send.at[3 + n], half_recv.at[3 + n],
            place.device(flip_xh=flip_xh, flip_xl=flip_xl),
        )

    def part_copy(d, part):
        target = lax.rem(z + d, 8)
        if part == 0:
            src, dst = part_a.at[target], in_a.at[d - 1]
        else:
            pair = pl.ds(2 * (part - 1), 2)
            src, dst = part_b.at[target, pair], in_b.at[d - 1, pair]
        n = part * 7 + d - 1
        return remote(src, dst, part_send.at[n], part_recv.at[n], place.device(dz=d))

    halves = [half_copy(n, *flips) for n, flips in enumerate(FLIPS)]
    lates = [late_copy(n, *flips) for n, flips in enumerate(FLIPS)]
    parts = [[part_copy(d, part) for d in ROUND] for part in range(3)]

    def start_towards(copies, half):
        for copy, (_, flip_xl) in zip(copies, FLIPS):
            to_xl = 1 - xl if flip_xl else xl
            pl.when(to_xl == half)(copy.start)

    def send_sums(part):
        first, count = (LOW_LANES, HIGH_LANES)[part]
        lanes = pl.ds(first, count)
        for n in range(2):
            rows = pl.ds(n * FF_PAD + A_ROWS, B_ROWS)
            turned_b[n, lanes] = jnp.transpose(head_term(part, 3, rows))
            for k in range(8):
                begin = (8 * part + k) * D_DEV
                part_b[k, 2 * part + n, 0:D_DEV] = turned_b[n, begin : begin + D_DEV].astype(BF16)
        for copy in parts[1 + part]:
            copy.start()
        for n in range(2):
            rows = pl.ds(n * FF_PAD, A_ROWS)
            total = head_term(part, 3, rows)
            head[rows, lanes] = total
            head_a[n, :, lanes] = total.astype(BF16)
        start_towards(halves, part)

    grds[0].got(*ORDER[3][1])
    send_sums(0)
    grds[1].near()
    add_head(1, 0)
    add_head(1, 1)
    add_head(1, 2)
    grds[1].far()
    far.send(0, 1, 2, 3)
    txt.pass_on()
    txt.near()
    grds[1].got(*ORDER[3][1])
    send_sums(1)

    visit_images(1, txt)
    visit_images(2, txt)
    txt.far()
    far.pass_on()
    visit_images(3, txt)

    for copy in halves:
        copy.wait_recv()
    total = head[pl.ds(pl.multiple_of(xh * FF_PAD, 16), A_ROWS), window(xl)]
    for n in range(3):
        total = total + head_in[n].astype(F32)
    turned[...] = jnp.transpose(total[0:128])
    row = lax.broadcasted_iota(jnp.int32, (256, 128), 0)
    column = lax.broadcasted_iota(jnp.int32, (256, 128), 1)
    rest = total[128:A_ROWS].astype(BF16)
    for n in range(8):
        rows = pl.ds(pl.multiple_of(n * D_DEV + xl * 64, 8), D_DEV)
        part_a[n, 0:D_DEV] = turned[rows].astype(BF16)
        first = min(n * D_DEV // 128 * 128, LANES - 256)
        shift = n * D_DEV - first + 64 * xl
        pick = jnp.where((row == column + shift) & (column < D_DEV), 1.0, 0.0).astype(BF16)
        part_a[n, 80:96] = jnp.dot(
            rest[:, first : first + 256], pick, preferred_element_type=F32
        ).astype(BF16)
    for copy in parts[0]:
        copy.start()

    far.near()
    for part in range(2):
        for copy in parts[1 + part]:
            copy.wait_recv()
        pair = slice(2 * part, 2 * part + 2)
        total = part_b[z, pair].astype(F32)
        for n in range(7):
            total = total + in_b[n, pair].astype(F32)
        sum_b[pair] = total.astype(BF16)
        start_towards(lates, part)

    visit_images(1, far)
    visit_images(2, far)
    far.far()
    visit_images(3, far)
    image_out[...] = unit_back(image_ref[...].astype(F32), image_sum[...])

    for copy in parts[0]:
        copy.wait_recv()
    total = part_a[z].astype(F32)
    for n in range(7):
        total = total + in_a[n].astype(F32)
    head_out[:, 0:128] = total[0:D_DEV]
    tail = jnp.concatenate([total[80:96], jnp.zeros((112, 128), F32)], axis=0)
    head_out[:, 256:FF_DEV] = jnp.transpose(tail)[0:D_DEV, 0 : FF_DEV - 256]
    for copy in lates:
        copy.wait_recv()
    total = sum_b[2 * xl + xh].astype(F32)
    for n in range(3):
        total = total + far_b[n].astype(F32)
    head_out[:, 128:256] = total[0:D_DEV]

    for gather in (img, txt, far, *grds):
        gather.finish()
    for copy in pieces + halves + lates + parts[0] + parts[1] + parts[2]:
        copy.wait_send()
    for copy in (text_across, text_back):
        copy.wait_send()


def settle(image_ref, head_ref, image_out, head_out):
    image_out[...] = image_ref[...]
    head_out[...] = head_ref[...]


def local(image_emb, text_hidden, head_weight, positive, log_scale, bias):
    vmem = pl.BlockSpec(memory_space=pltpu.VMEM)
    smem = pl.BlockSpec(memory_space=pltpu.SMEM)
    dma = pltpu.SemaphoreType.DMA
    sends = len(SENDS)
    image_grad, head_turned = pl.pallas_call(
        kernel,
        out_shape=(
            jax.ShapeDtypeStruct((ROWS, D), F32),
            jax.ShapeDtypeStruct((D_DEV, FF_DEV), F32),
        ),
        in_specs=[vmem, vmem, pl.BlockSpec(memory_space=pl.ANY), vmem, smem, smem],
        out_specs=(vmem, vmem),
        scratch_shapes=[
            pltpu.VMEM((FF, D), BF16),
            pltpu.VMEM((8, ROWS, D), BF16),
            pltpu.VMEM((8, ROWS, D), BF16),
            pltpu.VMEM((8, ROWS, D), BF16),
            pltpu.VMEM((8, ROWS, D), BF16),
            pltpu.VMEM((ROWS, D), F32),
            pltpu.VMEM((ROWS, D), F32),
            pltpu.VMEM((ROWS, D), F32),
            pltpu.VMEM((ROWS, D), F32),
            pltpu.VMEM((ROWS, D), BF16),
            pltpu.VMEM((ROWS, D), BF16),
            pltpu.VMEM((8, 2 * FF_PAD, ROWS), BF16),
            pltpu.VMEM((4, 2 * FF_PAD, 2 * ROWS), BF16),
            pltpu.VMEM((2 * FF_PAD, D), F32),
            pltpu.VMEM((2, A_ROWS, D), BF16),
            pltpu.VMEM((3, A_ROWS, LANES), BF16),
            pltpu.VMEM((LANES, 128), F32),
            pltpu.VMEM((2, D, 128), F32),
            pltpu.VMEM((8, 96, 128), BF16),
            pltpu.VMEM((8, 4, 80, 128), BF16),
            pltpu.VMEM((7, 96, 128), BF16),
            pltpu.VMEM((7, 4, 80, 128), BF16),
            pltpu.VMEM((4, 80, 128), BF16),
            pltpu.VMEM((3, 80, 128), BF16),
            dma((9,)),
            dma((sends,)),
            dma((sends,)),
            dma((sends,)),
            dma((sends,)),
            dma((sends,)),
            dma((sends,)),
            dma((sends,)),
            dma((sends,)),
            dma((sends,)),
            dma((sends,)),
            dma((2,)),
            dma((2,)),
            dma((7,)),
            dma((7,)),
            dma((6,)),
            dma((6,)),
            dma((21,)),
            dma((21,)),
        ],
        compiler_params=pltpu.CompilerParams(
            collective_id=0, has_side_effects=True, vmem_limit_bytes=60 * 1024 * 1024
        ),
    )(
        image_emb,
        text_hidden.T,
        head_weight,
        positive,
        log_scale,
        bias,
    )
    image_grad, head_turned = pl.pallas_call(
        settle,
        out_shape=(
            jax.ShapeDtypeStruct((ROWS, D), F32),
            jax.ShapeDtypeStruct((D_DEV, FF_DEV), F32),
        ),
        in_specs=[vmem, vmem],
        out_specs=(vmem, vmem),
        compiler_params=pltpu.CompilerParams(vmem_limit_bytes=60 * 1024 * 1024),
    )(image_grad, head_turned)
    return image_grad, head_turned.T


def solution(mesh):
    in_specs = (
        P(("grp", "blk"), None),
        P(("grp", "blk"), None),
        P(),
        P(("grp", "blk"), None),
        P(),
        P(),
    )
    out_specs = (P(("grp", "blk"), None), P("blk", "grp"))
    return jax.shard_map(local, mesh=mesh, in_specs=in_specs, out_specs=out_specs, check_vma=False)
```

```python
import jax
import jax.numpy as jnp
from jax import lax
from jax.experimental import pallas as pl
from jax.experimental.pallas import tpu as pltpu
from jax.sharding import PartitionSpec as P

MESH = pl.DeviceIdType.MESH
BF16 = jnp.bfloat16
F32 = jnp.float32

ROWS = 128
D = 1152
FF = 4304
FF_DEV = 269
FF_PAD = 272
WINDOW = 288
D_DEV = 72
LANES = 640
CHUNK = 512
A_ROWS, B_ROWS = 144, 128
LOW_LANES, HIGH_LANES = (0, LANES), (LANES, D - LANES)


def nt_dot(left, right):
    return lax.dot_general(left, right, (((1,), (1,)), ((), ())), preferred_element_type=F32)


def tn_dot(left, right):
    return lax.dot_general(left, right, (((0,), (0,)), ((), ())), preferred_element_type=F32)


class Place:
    def __init__(self):
        self.g = lax.axis_index("grp")
        self.b = lax.axis_index("blk")
        rest = lax.rem(self.b, 4)
        self.y, self.xh, self.c = lax.div(self.b, 4), lax.div(rest, 2), lax.rem(rest, 2)
        self.xl, self.z = lax.div(self.g, 8), lax.rem(self.g, 8)

    def slot(self, dy, flip_c):
        return self.turn(dy) * 2 + (1 - self.c if flip_c else self.c)

    def turn(self, dy):
        return lax.rem(self.y + dy, 4)

    def device(self, dy=0, flip_c=0, flip_xh=0, flip_xl=0, dz=0):
        c = 1 - self.c if flip_c else self.c
        xh = 1 - self.xh if flip_xh else self.xh
        xl = 1 - self.xl if flip_xl else self.xl
        return (xl * 8 + lax.rem(self.z + dz, 8), self.turn(dy) * 4 + xh * 2 + c)


FULL, LOW, HIGH = (0, ROWS), (0, ROWS // 2), (ROWS // 2, ROWS // 2)
OWN, UP, DOWN, FAR, TWIN = (0, 0), (1, 0), (3, 0), (2, 0), (0, 1)
SENDS = [
    (OWN, LOW, UP, DOWN),
    (OWN, HIGH, DOWN, UP),
    (OWN, HIGH, UP, DOWN),
    (OWN, LOW, DOWN, UP),
    (DOWN, LOW, UP, FAR),
    (UP, HIGH, DOWN, FAR),
    (OWN, FULL, TWIN, TWIN),
    (DOWN, FULL, TWIN, (3, 1)),
    (UP, FULL, TWIN, (1, 1)),
    (FAR, LOW, TWIN, (2, 1)),
    (FAR, HIGH, TWIN, (2, 1)),
]
ORDER = [(0, (6,)), (3, (7,)), (1, (8,)), (2, (9, 10))]


class Gather:
    def __init__(self, place, buf, send_sem, recv_sem, lanes=(0, D)):
        self.place, self.buf, self.send_sem, self.recv_sem = place, buf, send_sem, recv_sem
        self.lanes = pl.ds(*lanes)
        self.held = []

    def copy(self, i, block):
        _, (first, count), target, _ = SENDS[i]
        ref = self.buf.at[self.place.slot(*block), pl.ds(first, count), self.lanes]
        return pltpu.make_async_remote_copy(
            src_ref=ref,
            dst_ref=ref,
            send_sem=self.send_sem.at[i],
            recv_sem=self.recv_sem.at[i],
            device_id=self.place.device(*target),
            device_id_type=MESH,
        )

    def send(self, *which):
        for i in which:
            copy = self.copy(i, SENDS[i][0])
            copy.start()
            self.held.append(copy)

    def got(self, *which):
        for i in which:
            self.copy(i, SENDS[i][3]).wait_recv()

    def pass_on(self):
        self.got(0)
        self.send(4)
        self.got(1)
        self.send(5)

    def near(self):
        self.got(2)
        self.send(7)
        self.got(3)
        self.send(8)

    def far(self):
        self.got(4)
        self.send(9)
        self.got(5)
        self.send(10)

    def finish(self):
        for copy in self.held:
            copy.wait_send()


def kernel(
    image_ref, hidden_ref, weight_ref, positive_ref, scale_ref, bias_ref,
    image_out, head_out,
    weight_buf, images, texts, grads, far_image, far_text, raw, text_sum, image_sum, far_sum,
    text_back_out, text_back_in, image_back_out, image_back_in,
    piece_out, piece_in, head, head_a, head_in, turned, turned_b,
    part_a, part_b, in_a, in_b, sum_b, far_b,
    weight_sem, img_send, img_recv, txt_send, txt_recv,
    low_send, low_recv, high_send, high_recv,
    x_send, x_recv, hid_send, hid_recv, half_send, half_recv, part_send, part_recv,
):
    place = Place()
    y, c, xh, xl, z = place.y, place.c, place.xh, place.xl, place.z
    own = place.slot(*OWN)

    barrier = pltpu.get_barrier_semaphore()
    peers = [place.device(dy, fc) for dy in range(4) for fc in range(2) if dy or fc]
    peers += [place.device(flip_xh=1), place.device(flip_xl=1), place.device(flip_xh=1, flip_xl=1)]
    peers += [place.device(dz=d) for d in range(1, 8)]
    for peer in peers:
        pl.semaphore_signal(barrier, inc=1, device_id=peer, device_id_type=MESH)

    bounds = [(k, min(CHUNK, FF - k)) for k in range(0, FF, CHUNK)]
    weight_copies = []
    for n, (first, count) in enumerate(bounds):
        rows = pl.ds(first, count)
        copy = pltpu.make_async_copy(weight_ref.at[rows], weight_buf.at[rows], weight_sem.at[n])
        copy.start()
        weight_copies.append(copy)

    def unit_of(values):
        norm = jnp.sqrt(jnp.sum(values * values, axis=-1, keepdims=True) + 1e-06)
        return norm, values / norm

    def unit_back(values, incoming):
        norm, direction = unit_of(values)
        along = jnp.sum(direction * incoming, axis=-1, keepdims=True)
        return (incoming - direction * along) / norm

    def remote(src, dst, send_sem, recv_sem, target):
        return pltpu.make_async_remote_copy(
            src_ref=src,
            dst_ref=dst,
            send_sem=send_sem,
            recv_sem=recv_sem,
            device_id=target,
            device_id_type=MESH,
        )

    img = Gather(place, images, img_send, img_recv)
    txt = Gather(place, texts, txt_send, txt_recv)
    grds = [
        Gather(place, grads, low_send, low_recv, LOW_LANES),
        Gather(place, grads, high_send, high_recv, HIGH_LANES),
    ]
    partner = place.device(flip_xh=1)

    def across(n, src, dst):
        return remote(src, dst, x_send.at[n], x_recv.at[n], partner)

    text_across = across(0, texts.at[own], far_text)
    text_back = across(1, text_back_out, text_back_in)
    image_across = across(2, images.at[own], far_image)
    image_back = across(3, image_back_out, image_back_in)

    def cut(start, first, window):
        row = lax.broadcasted_iota(jnp.int32, (FF_PAD, window), 0)
        column = lax.broadcasted_iota(jnp.int32, (FF_PAD, window), 1)
        wanted = jnp.where(row < 128, row, jnp.where(row < A_ROWS, row + 128, row - 16))
        pick = jnp.where(column == wanted + (start - first), 1.0, 0.0).astype(BF16)
        return jnp.dot(
            pick, hidden_ref[pl.ds(first, window)], preferred_element_type=F32
        ).astype(BF16)

    def cut_step(n, carry):
        start = n * FF_DEV
        first = pl.multiple_of(lax.div(start, 16) * 16, 16)
        column, half = lax.div(n, 4) * 2 + lax.rem(n, 2), lax.rem(lax.div(n, 2), 2)
        rows = pl.ds(pl.multiple_of(half * FF_PAD, 16), FF_PAD)
        piece_out[column, rows] = cut(start, first, WINDOW)
        return carry

    images[own] = unit_of(image_ref[...].astype(F32))[1].astype(BF16)
    lax.fori_loop(0, 5, cut_step, 0)
    pl.semaphore_wait(barrier, len(peers))
    img.send(0, 1, 6)
    lax.fori_loop(5, 11, cut_step, 0)
    img.send(2, 3)
    lax.fori_loop(11, 15, cut_step, 0)
    last = 15 * FF_DEV
    piece_out[7, FF_PAD : 2 * FF_PAD] = cut(last, last // 16 * 16, FF - last // 16 * 16)

    for n, (first, count) in enumerate(bounds):
        weight_copies[n].wait()
        rows = pl.ds(first, count)
        term = tn_dot(hidden_ref[rows], weight_buf[rows])
        raw[...] = term if n == 0 else raw[...] + term
    texts[own] = unit_of(raw[...])[1].astype(BF16)
    text_across.start()
    txt.send(6)
    img.pass_on()

    def lane(core):
        return pl.ds(pl.multiple_of(core * ROWS, ROWS), ROWS)

    OTHERS = [(dy, fc) for dy in (1, 3, 2) for fc in range(2)] + [TWIN]

    def piece_copy(n, dy, fc, back=False):
        if back:
            dst = piece_in.at[place.turn(4 - dy), :, lane(1 - c if fc else c)]
        else:
            dst = piece_in.at[y, :, lane(c)]
        return remote(
            piece_out.at[place.slot(dy, fc)], dst, hid_send.at[n], hid_recv.at[n],
            place.device(dy, fc),
        )

    pieces = [piece_copy(n, *target) for n, target in enumerate(OTHERS)]
    piece_in[y, :, lane(c)] = piece_out[own]
    img.near()
    for copy in pieces:
        copy.start()

    logit_scale = jnp.exp(jnp.full((1, 2 * ROWS), scale_ref[0], F32))
    logit_bias = bias_ref[0]
    text_row = lax.broadcasted_iota(jnp.int32, (ROWS, ROWS), 0)
    label = jnp.where(text_row == positive_ref[...], 1.0, 0.0)

    def with_twin(value):
        return jnp.concatenate(
            [jnp.where(c == 0, value, 0.0), jnp.where(c == 0, 0.0, value)], axis=1
        )

    def chip(buf, dy):
        return buf[pl.ds(2 * place.turn(dy), 2)].reshape(2 * ROWS, D)

    def visit(unit, block, total, first, own_label=None):
        chance = jax.nn.sigmoid(logit_scale * nt_dot(unit, block) + logit_bias)
        if own_label is not None:
            chance = chance - with_twin(own_label)
        weight = (logit_scale * chance).astype(BF16)
        term = jnp.dot(weight, block, preferred_element_type=F32)
        total[...] = term if first else total[...] + term

    def visit_texts(n):
        label_of = label if n == 0 else None
        visit(texts[own], chip(images, ORDER[n][0]), text_sum, n == 0, label_of)

    def visit_far_texts(n):
        visit(far_text[...], chip(images, ORDER[n][0]), far_sum, n == 0)

    def visit_images(n):
        txt.got(*ORDER[n][1])
        own_label = jnp.transpose(label) if n == 0 else None
        visit(images[own], chip(texts, ORDER[n][0]), image_sum, n == 0, own_label)

    def visit_far_images(n):
        visit(far_image[...], chip(texts, ORDER[n][0]), far_sum, n == 0)

    for n in range(3):
        img.got(*ORDER[n][1])
        visit_texts(n)
    img.far()
    txt.send(0, 1, 2, 3)
    text_across.wait_recv()
    for n in range(3):
        visit_far_texts(n)
    img.got(*ORDER[3][1])
    visit_far_texts(3)
    text_back_out[...] = far_sum[...].astype(BF16)
    text_back.start()
    visit_texts(3)
    visit_images(0)
    text_back.wait_recv()
    incoming = text_sum[...] + text_back_in[...].astype(F32)
    grads[own] = unit_back(raw[...], incoming).astype(BF16)
    grds[0].send(0, 1, 2, 3, 6)
    image_across.start()
    for n, (dy, fc) in enumerate(OTHERS):
        piece_copy(n, dy, fc, back=True).wait_recv()

    def head_term(part, n, rows):
        first, count = (LOW_LANES, HIGH_LANES)[part]
        lanes = pl.ds(first, count)
        turn = place.turn(ORDER[n][0])
        block = grads[pl.ds(2 * turn, 2), :, lanes].reshape(2 * ROWS, count)
        term = jnp.dot(piece_in[turn, rows], block, preferred_element_type=F32)
        return term if n == 0 else head[rows, lanes] + term

    def add_head(part, n):
        grds[part].got(*ORDER[n][1])
        head[:, pl.ds(*(LOW_LANES, HIGH_LANES)[part])] = head_term(part, n, pl.ds(0, 2 * FF_PAD))

    add_head(0, 0)
    grds[0].pass_on()
    grds[1].send(0, 1, 2, 3, 6)
    grds[0].near()
    add_head(0, 1)
    add_head(0, 2)
    grds[0].far()
    grds[1].pass_on()

    FLIPS = [(0, 1), (1, 0), (1, 1)]
    ROUND = (1, 7, 2, 6, 3, 5, 4)

    def window(half):
        return pl.ds(pl.multiple_of(half * 512, 128), LANES)

    def half_copy(n, flip_xh, flip_xl):
        to_xh = 1 - xh if flip_xh else xh
        to_xl = 1 - xl if flip_xl else xl
        return remote(
            head_a.at[to_xh, :, window(to_xl)], head_in.at[n], half_send.at[n], half_recv.at[n],
            place.device(flip_xh=flip_xh, flip_xl=flip_xl),
        )

    def late_copy(n, flip_xh, flip_xl):
        to_xh = 1 - xh if flip_xh else xh
        to_xl = 1 - xl if flip_xl else xl
        return remote(
            sum_b.at[2 * to_xl + to_xh], far_b.at[n], half_send.at[3 + n], half_recv.at[3 + n],
            place.device(flip_xh=flip_xh, flip_xl=flip_xl),
        )

    def part_copy(d, part):
        target = lax.rem(z + d, 8)
        if part == 0:
            src, dst = part_a.at[target], in_a.at[d - 1]
        else:
            pair = pl.ds(2 * (part - 1), 2)
            src, dst = part_b.at[target, pair], in_b.at[d - 1, pair]
        n = part * 7 + d - 1
        return remote(src, dst, part_send.at[n], part_recv.at[n], place.device(dz=d))

    halves = [half_copy(n, *flips) for n, flips in enumerate(FLIPS)]
    lates = [late_copy(n, *flips) for n, flips in enumerate(FLIPS)]
    parts = [[part_copy(d, part) for d in ROUND] for part in range(3)]

    def start_towards(copies, half):
        for copy, (_, flip_xl) in zip(copies, FLIPS):
            to_xl = 1 - xl if flip_xl else xl
            pl.when(to_xl == half)(copy.start)

    def send_sums(part):
        first, count = (LOW_LANES, HIGH_LANES)[part]
        lanes = pl.ds(first, count)
        for n in range(2):
            rows = pl.ds(n * FF_PAD + A_ROWS, B_ROWS)
            turned_b[n, lanes] = jnp.transpose(head_term(part, 3, rows))
            for k in range(8):
                begin = (8 * part + k) * D_DEV
                part_b[k, 2 * part + n, 0:D_DEV] = turned_b[n, begin : begin + D_DEV].astype(BF16)
        for copy in parts[1 + part]:
            copy.start()
        for n in range(2):
            rows = pl.ds(n * FF_PAD, A_ROWS)
            total = head_term(part, 3, rows)
            head[rows, lanes] = total
            head_a[n, :, lanes] = total.astype(BF16)
        start_towards(halves, part)

    grds[0].got(*ORDER[3][1])
    send_sums(0)
    image_across.wait_recv()
    visit_far_images(0)
    grds[1].near()
    add_head(1, 0)
    add_head(1, 1)
    add_head(1, 2)
    grds[1].far()
    txt.pass_on()
    txt.near()
    grds[1].got(*ORDER[3][1])
    send_sums(1)

    for n in (1, 2):
        visit_images(n)
        visit_far_images(n)
    txt.far()
    visit_images(3)
    visit_far_images(3)
    image_back_out[...] = far_sum[...].astype(BF16)
    image_back.start()

    for copy in halves:
        copy.wait_recv()
    total = head[pl.ds(pl.multiple_of(xh * FF_PAD, 16), A_ROWS), window(xl)]
    for n in range(3):
        total = total + head_in[n].astype(F32)
    turned[...] = jnp.transpose(total[0:128])
    row = lax.broadcasted_iota(jnp.int32, (256, 128), 0)
    column = lax.broadcasted_iota(jnp.int32, (256, 128), 1)
    rest = total[128:A_ROWS].astype(BF16)
    for n in range(8):
        rows = pl.ds(pl.multiple_of(n * D_DEV + xl * 64, 8), D_DEV)
        part_a[n, 0:D_DEV] = turned[rows].astype(BF16)
        first = min(n * D_DEV // 128 * 128, LANES - 256)
        shift = n * D_DEV - first + 64 * xl
        pick = jnp.where((row == column + shift) & (column < D_DEV), 1.0, 0.0).astype(BF16)
        part_a[n, 80:96] = jnp.dot(
            rest[:, first : first + 256], pick, preferred_element_type=F32
        ).astype(BF16)
    for copy in parts[0]:
        copy.start()

    for part in range(2):
        for copy in parts[1 + part]:
            copy.wait_recv()
        pair = slice(2 * part, 2 * part + 2)
        total = part_b[z, pair].astype(F32)
        for n in range(7):
            total = total + in_b[n, pair].astype(F32)
        sum_b[pair] = total.astype(BF16)
        start_towards(lates, part)

    image_back.wait_recv()
    incoming = image_sum[...] + image_back_in[...].astype(F32)
    image_out[...] = unit_back(image_ref[...].astype(F32), incoming)

    for copy in parts[0]:
        copy.wait_recv()
    total = part_a[z].astype(F32)
    for n in range(7):
        total = total + in_a[n].astype(F32)
    head_out[:, 0:128] = total[0:D_DEV]
    tail = jnp.concatenate([total[80:96], jnp.zeros((112, 128), F32)], axis=0)
    head_out[:, 256:FF_DEV] = jnp.transpose(tail)[0:D_DEV, 0 : FF_DEV - 256]
    for copy in lates:
        copy.wait_recv()
    total = sum_b[2 * xl + xh].astype(F32)
    for n in range(3):
        total = total + far_b[n].astype(F32)
    head_out[:, 128:256] = total[0:D_DEV]

    for gather in (img, txt, *grds):
        gather.finish()
    for copy in pieces + halves + lates + parts[0] + parts[1] + parts[2]:
        copy.wait_send()
    for copy in (text_across, text_back, image_across, image_back):
        copy.wait_send()


def settle(image_ref, head_ref, image_out, head_out):
    image_out[...] = image_ref[...]
    head_out[...] = head_ref[...]


def local(image_emb, text_hidden, head_weight, positive, log_scale, bias):
    vmem = pl.BlockSpec(memory_space=pltpu.VMEM)
    smem = pl.BlockSpec(memory_space=pltpu.SMEM)
    dma = pltpu.SemaphoreType.DMA
    sends = len(SENDS)
    image_grad, head_turned = pl.pallas_call(
        kernel,
        out_shape=(
            jax.ShapeDtypeStruct((ROWS, D), F32),
            jax.ShapeDtypeStruct((D_DEV, FF_DEV), F32),
        ),
        in_specs=[vmem, vmem, pl.BlockSpec(memory_space=pl.ANY), vmem, smem, smem],
        out_specs=(vmem, vmem),
        scratch_shapes=[
            pltpu.VMEM((FF, D), BF16),
            pltpu.VMEM((8, ROWS, D), BF16),
            pltpu.VMEM((8, ROWS, D), BF16),
            pltpu.VMEM((8, ROWS, D), BF16),
            pltpu.VMEM((ROWS, D), BF16),
            pltpu.VMEM((ROWS, D), BF16),
            pltpu.VMEM((ROWS, D), F32),
            pltpu.VMEM((ROWS, D), F32),
            pltpu.VMEM((ROWS, D), F32),
            pltpu.VMEM((ROWS, D), F32),
            pltpu.VMEM((ROWS, D), BF16),
            pltpu.VMEM((ROWS, D), BF16),
            pltpu.VMEM((ROWS, D), BF16),
            pltpu.VMEM((ROWS, D), BF16),
            pltpu.VMEM((8, 2 * FF_PAD, ROWS), BF16),
            pltpu.VMEM((4, 2 * FF_PAD, 2 * ROWS), BF16),
            pltpu.VMEM((2 * FF_PAD, D), F32),
            pltpu.VMEM((2, A_ROWS, D), BF16),
            pltpu.VMEM((3, A_ROWS, LANES), BF16),
            pltpu.VMEM((LANES, 128), F32),
            pltpu.VMEM((2, D, 128), F32),
            pltpu.VMEM((8, 96, 128), BF16),
            pltpu.VMEM((8, 4, 80, 128), BF16),
            pltpu.VMEM((7, 96, 128), BF16),
            pltpu.VMEM((7, 4, 80, 128), BF16),
            pltpu.VMEM((4, 80, 128), BF16),
            pltpu.VMEM((3, 80, 128), BF16),
            dma((9,)),
            dma((sends,)),
            dma((sends,)),
            dma((sends,)),
            dma((sends,)),
            dma((sends,)),
            dma((sends,)),
            dma((sends,)),
            dma((sends,)),
            dma((4,)),
            dma((4,)),
            dma((7,)),
            dma((7,)),
            dma((6,)),
            dma((6,)),
            dma((21,)),
            dma((21,)),
        ],
        compiler_params=pltpu.CompilerParams(
            collective_id=0, has_side_effects=True, vmem_limit_bytes=60 * 1024 * 1024
        ),
    )(
        image_emb,
        text_hidden.T,
        head_weight,
        positive,
        log_scale,
        bias,
    )
    image_grad, head_turned = pl.pallas_call(
        settle,
        out_shape=(
            jax.ShapeDtypeStruct((ROWS, D), F32),
            jax.ShapeDtypeStruct((D_DEV, FF_DEV), F32),
        ),
        in_specs=[vmem, vmem],
        out_specs=(vmem, vmem),
        compiler_params=pltpu.CompilerParams(vmem_limit_bytes=60 * 1024 * 1024),
    )(image_grad, head_turned)
    return image_grad, head_turned.T


def solution(mesh):
    in_specs = (
        P(("grp", "blk"), None),
        P(("grp", "blk"), None),
        P(),
        P(("grp", "blk"), None),
        P(),
        P(),
    )
    out_specs = (P(("grp", "blk"), None), P("blk", "grp"))
    return jax.shard_map(local, mesh=mesh, in_specs=in_specs, out_specs=out_specs, check_vma=False)
```

```python
import jax
import jax.numpy as jnp
from jax import lax
from jax.experimental import pallas as pl
from jax.experimental.pallas import tpu as pltpu
from jax.sharding import PartitionSpec as P

MESH = pl.DeviceIdType.MESH
BF16 = jnp.bfloat16
F32 = jnp.float32

ROWS = 128
D = 1152
FF = 4304
FF_DEV = 269
FF_PAD = 272
WINDOW = 288
D_DEV = 72
LANES = 640
CHUNK = 512
A_ROWS, B_ROWS = 144, 128
LOW_LANES, HIGH_LANES = (0, LANES), (LANES, D - LANES)


def nt_dot(left, right):
    return lax.dot_general(left, right, (((1,), (1,)), ((), ())), preferred_element_type=F32)


def tn_dot(left, right):
    return lax.dot_general(left, right, (((0,), (0,)), ((), ())), preferred_element_type=F32)


class Place:
    def __init__(self):
        self.g = lax.axis_index("grp")
        self.b = lax.axis_index("blk")
        rest = lax.rem(self.b, 4)
        self.y, self.xh, self.c = lax.div(self.b, 4), lax.div(rest, 2), lax.rem(rest, 2)
        self.xl, self.z = lax.div(self.g, 8), lax.rem(self.g, 8)

    def slot(self, dy, flip_c):
        return self.turn(dy) * 2 + (1 - self.c if flip_c else self.c)

    def turn(self, dy):
        return lax.rem(self.y + dy, 4)

    def device(self, dy=0, flip_c=0, flip_xh=0, flip_xl=0, dz=0):
        c = 1 - self.c if flip_c else self.c
        xh = 1 - self.xh if flip_xh else self.xh
        xl = 1 - self.xl if flip_xl else self.xl
        return (xl * 8 + lax.rem(self.z + dz, 8), self.turn(dy) * 4 + xh * 2 + c)


FULL, LOW, HIGH = (0, ROWS), (0, ROWS // 2), (ROWS // 2, ROWS // 2)
OWN, UP, DOWN, FAR, TWIN = (0, 0), (1, 0), (3, 0), (2, 0), (0, 1)
SENDS = [
    (OWN, LOW, UP, DOWN),
    (OWN, HIGH, DOWN, UP),
    (OWN, HIGH, UP, DOWN),
    (OWN, LOW, DOWN, UP),
    (DOWN, LOW, UP, FAR),
    (UP, HIGH, DOWN, FAR),
    (OWN, FULL, TWIN, TWIN),
    (DOWN, FULL, TWIN, (3, 1)),
    (UP, FULL, TWIN, (1, 1)),
    (FAR, LOW, TWIN, (2, 1)),
    (FAR, HIGH, TWIN, (2, 1)),
]
ORDER = [(0, (6,)), (3, (7,)), (1, (8,)), (2, (9, 10))]


class Gather:
    def __init__(self, place, buf, send_sem, recv_sem, lanes=(0, D)):
        self.place, self.buf, self.send_sem, self.recv_sem = place, buf, send_sem, recv_sem
        self.lanes = pl.ds(*lanes)
        self.held = []

    def copy(self, i, block):
        _, (first, count), target, _ = SENDS[i]
        ref = self.buf.at[self.place.slot(*block), pl.ds(first, count), self.lanes]
        return pltpu.make_async_remote_copy(
            src_ref=ref,
            dst_ref=ref,
            send_sem=self.send_sem.at[i],
            recv_sem=self.recv_sem.at[i],
            device_id=self.place.device(*target),
            device_id_type=MESH,
        )

    def send(self, *which):
        for i in which:
            copy = self.copy(i, SENDS[i][0])
            copy.start()
            self.held.append(copy)

    def got(self, *which):
        for i in which:
            self.copy(i, SENDS[i][3]).wait_recv()

    def pass_on(self):
        self.got(0)
        self.send(4)
        self.got(1)
        self.send(5)

    def near(self):
        self.got(2)
        self.send(7)
        self.got(3)
        self.send(8)

    def far(self):
        self.got(4)
        self.send(9)
        self.got(5)
        self.send(10)

    def finish(self):
        for copy in self.held:
            copy.wait_send()


def kernel(
    image_ref, hidden_ref, weight_ref, positive_ref, scale_ref, bias_ref,
    image_out, head_out,
    weight_buf, images, texts, far_texts, grads, raw, text_sum, image_sum, far_sum,
    text_back_out, text_back_in,
    piece_out, piece_in, head, head_a, head_in, turned, turned_b,
    part_a, part_b, in_a, in_b, sum_b, far_b,
    weight_sem, img_send, img_recv, txt_send, txt_recv, far_send, far_recv,
    low_send, low_recv, high_send, high_recv,
    x_send, x_recv, hid_send, hid_recv, half_send, half_recv, part_send, part_recv,
):
    place = Place()
    y, c, xh, xl, z = place.y, place.c, place.xh, place.xl, place.z
    own = place.slot(*OWN)

    barrier = pltpu.get_barrier_semaphore()
    peers = [place.device(dy, fc) for dy in range(4) for fc in range(2) if dy or fc]
    peers += [place.device(flip_xh=1), place.device(flip_xl=1), place.device(flip_xh=1, flip_xl=1)]
    peers += [place.device(dz=d) for d in range(1, 8)]
    for peer in peers:
        pl.semaphore_signal(barrier, inc=1, device_id=peer, device_id_type=MESH)

    bounds = [(k, min(CHUNK, FF - k)) for k in range(0, FF, CHUNK)]
    weight_copies = []
    for n, (first, count) in enumerate(bounds):
        rows = pl.ds(first, count)
        copy = pltpu.make_async_copy(weight_ref.at[rows], weight_buf.at[rows], weight_sem.at[n])
        copy.start()
        weight_copies.append(copy)

    def unit_of(values):
        norm = jnp.sqrt(jnp.sum(values * values, axis=-1, keepdims=True) + 1e-06)
        return norm, values / norm

    def unit_back(values, incoming):
        norm, direction = unit_of(values)
        along = jnp.sum(direction * incoming, axis=-1, keepdims=True)
        return (incoming - direction * along) / norm

    def remote(src, dst, send_sem, recv_sem, target):
        return pltpu.make_async_remote_copy(
            src_ref=src,
            dst_ref=dst,
            send_sem=send_sem,
            recv_sem=recv_sem,
            device_id=target,
            device_id_type=MESH,
        )

    img = Gather(place, images, img_send, img_recv)
    txt = Gather(place, texts, txt_send, txt_recv)
    far = Gather(place, far_texts, far_send, far_recv)
    grds = [
        Gather(place, grads, low_send, low_recv, LOW_LANES),
        Gather(place, grads, high_send, high_recv, HIGH_LANES),
    ]
    partner = place.device(flip_xh=1)

    def across(n, src, dst):
        return remote(src, dst, x_send.at[n], x_recv.at[n], partner)

    text_across = across(0, texts.at[own], far_texts.at[own])
    text_back = across(1, text_back_out, text_back_in)

    def cut(start, first, window):
        row = lax.broadcasted_iota(jnp.int32, (FF_PAD, window), 0)
        column = lax.broadcasted_iota(jnp.int32, (FF_PAD, window), 1)
        wanted = jnp.where(row < 128, row, jnp.where(row < A_ROWS, row + 128, row - 16))
        pick = jnp.where(column == wanted + (start - first), 1.0, 0.0).astype(BF16)
        return jnp.dot(
            pick, hidden_ref[pl.ds(first, window)], preferred_element_type=F32
        ).astype(BF16)

    def cut_step(n, carry):
        start = n * FF_DEV
        first = pl.multiple_of(lax.div(start, 16) * 16, 16)
        column, half = lax.div(n, 4) * 2 + lax.rem(n, 2), lax.rem(lax.div(n, 2), 2)
        rows = pl.ds(pl.multiple_of(half * FF_PAD, 16), FF_PAD)
        piece_out[column, rows] = cut(start, first, WINDOW)
        return carry

    images[own] = unit_of(image_ref[...].astype(F32))[1].astype(BF16)
    lax.fori_loop(0, 5, cut_step, 0)
    pl.semaphore_wait(barrier, len(peers))
    img.send(0, 1, 6)
    lax.fori_loop(5, 11, cut_step, 0)
    img.send(2, 3)
    lax.fori_loop(11, 15, cut_step, 0)
    last = 15 * FF_DEV
    piece_out[7, FF_PAD : 2 * FF_PAD] = cut(last, last // 16 * 16, FF - last // 16 * 16)

    for n, (first, count) in enumerate(bounds):
        weight_copies[n].wait()
        rows = pl.ds(first, count)
        term = tn_dot(hidden_ref[rows], weight_buf[rows])
        raw[...] = term if n == 0 else raw[...] + term
    texts[own] = unit_of(raw[...])[1].astype(BF16)
    text_across.start()
    txt.send(6)
    img.pass_on()

    def lane(core):
        return pl.ds(pl.multiple_of(core * ROWS, ROWS), ROWS)

    OTHERS = [(dy, fc) for dy in (1, 3, 2) for fc in range(2)] + [TWIN]

    def piece_copy(n, dy, fc, back=False):
        if back:
            dst = piece_in.at[place.turn(4 - dy), :, lane(1 - c if fc else c)]
        else:
            dst = piece_in.at[y, :, lane(c)]
        return remote(
            piece_out.at[place.slot(dy, fc)], dst, hid_send.at[n], hid_recv.at[n],
            place.device(dy, fc),
        )

    pieces = [piece_copy(n, *target) for n, target in enumerate(OTHERS)]
    piece_in[y, :, lane(c)] = piece_out[own]
    img.near()
    for copy in pieces:
        copy.start()

    logit_scale = jnp.exp(jnp.full((1, 2 * ROWS), scale_ref[0], F32))
    logit_bias = bias_ref[0]
    text_row = lax.broadcasted_iota(jnp.int32, (ROWS, ROWS), 0)
    label = jnp.where(text_row == positive_ref[...], 1.0, 0.0)

    def with_twin(value):
        return jnp.concatenate(
            [jnp.where(c == 0, value, 0.0), jnp.where(c == 0, 0.0, value)], axis=1
        )

    def chip(buf, dy):
        return buf[pl.ds(2 * place.turn(dy), 2)].reshape(2 * ROWS, D)

    def visit(unit, block, total, first, own_label=None):
        chance = jax.nn.sigmoid(logit_scale * nt_dot(unit, block) + logit_bias)
        if own_label is not None:
            chance = chance - with_twin(own_label)
        weight = (logit_scale * chance).astype(BF16)
        term = jnp.dot(weight, block, preferred_element_type=F32)
        total[...] = term if first else total[...] + term

    def visit_texts(n):
        label_of = label if n == 0 else None
        visit(texts[own], chip(images, ORDER[n][0]), text_sum, n == 0, label_of)

    def visit_far_texts(n):
        visit(far_texts[own], chip(images, ORDER[n][0]), far_sum, n == 0)

    def visit_images(n, gather):
        gather.got(*ORDER[n][1])
        own_label = jnp.transpose(label) if n == 0 and gather is txt else None
        block = chip(gather.buf, ORDER[n][0])
        visit(images[own], block, image_sum, own_label is not None, own_label)

    for n in range(3):
        img.got(*ORDER[n][1])
        visit_texts(n)
    img.far()
    text_across.wait_recv()
    far.send(6)
    for n in range(3):
        visit_far_texts(n)
    img.got(*ORDER[3][1])
    visit_far_texts(3)
    text_back_out[...] = far_sum[...].astype(BF16)
    text_back.start()
    txt.send(0, 1, 2, 3)
    visit_texts(3)
    visit_images(0, txt)
    visit_images(0, far)
    text_back.wait_recv()
    incoming = text_sum[...] + text_back_in[...].astype(F32)
    grads[own] = unit_back(raw[...], incoming).astype(BF16)
    grds[0].send(0, 1, 2, 3, 6)
    for n, (dy, fc) in enumerate(OTHERS):
        piece_copy(n, dy, fc, back=True).wait_recv()

    def head_term(part, n, rows):
        first, count = (LOW_LANES, HIGH_LANES)[part]
        lanes = pl.ds(first, count)
        turn = place.turn(ORDER[n][0])
        block = grads[pl.ds(2 * turn, 2), :, lanes].reshape(2 * ROWS, count)
        term = jnp.dot(piece_in[turn, rows], block, preferred_element_type=F32)
        return term if n == 0 else head[rows, lanes] + term

    def add_head(part, n):
        grds[part].got(*ORDER[n][1])
        head[:, pl.ds(*(LOW_LANES, HIGH_LANES)[part])] = head_term(part, n, pl.ds(0, 2 * FF_PAD))

    add_head(0, 0)
    grds[0].pass_on()
    grds[1].send(0, 1, 2, 3, 6)
    grds[0].near()
    add_head(0, 1)
    add_head(0, 2)
    grds[0].far()
    grds[1].pass_on()

    FLIPS = [(0, 1), (1, 0), (1, 1)]
    ROUND = (1, 7, 2, 6, 3, 5, 4)

    def window(half):
        return pl.ds(pl.multiple_of(half * 512, 128), LANES)

    def half_copy(n, flip_xh, flip_xl):
        to_xh = 1 - xh if flip_xh else xh
        to_xl = 1 - xl if flip_xl else xl
        return remote(
            head_a.at[to_xh, :, window(to_xl)], head_in.at[n], half_send.at[n], half_recv.at[n],
            place.device(flip_xh=flip_xh, flip_xl=flip_xl),
        )

    def late_copy(n, flip_xh, flip_xl):
        to_xh = 1 - xh if flip_xh else xh
        to_xl = 1 - xl if flip_xl else xl
        return remote(
            sum_b.at[2 * to_xl + to_xh], far_b.at[n], half_send.at[3 + n], half_recv.at[3 + n],
            place.device(flip_xh=flip_xh, flip_xl=flip_xl),
        )

    def part_copy(d, part):
        target = lax.rem(z + d, 8)
        if part == 0:
            src, dst = part_a.at[target], in_a.at[d - 1]
        else:
            pair = pl.ds(2 * (part - 1), 2)
            src, dst = part_b.at[target, pair], in_b.at[d - 1, pair]
        n = part * 7 + d - 1
        return remote(src, dst, part_send.at[n], part_recv.at[n], place.device(dz=d))

    halves = [half_copy(n, *flips) for n, flips in enumerate(FLIPS)]
    lates = [late_copy(n, *flips) for n, flips in enumerate(FLIPS)]
    parts = [[part_copy(d, part) for d in ROUND] for part in range(3)]

    def start_towards(copies, half):
        for copy, (_, flip_xl) in zip(copies, FLIPS):
            to_xl = 1 - xl if flip_xl else xl
            pl.when(to_xl == half)(copy.start)

    def send_sums(part):
        first, count = (LOW_LANES, HIGH_LANES)[part]
        lanes = pl.ds(first, count)
        for n in range(2):
            rows = pl.ds(n * FF_PAD + A_ROWS, B_ROWS)
            turned_b[n, lanes] = jnp.transpose(head_term(part, 3, rows))
            for k in range(8):
                begin = (8 * part + k) * D_DEV
                part_b[k, 2 * part + n, 0:D_DEV] = turned_b[n, begin : begin + D_DEV].astype(BF16)
        for copy in parts[1 + part]:
            copy.start()
        for n in range(2):
            rows = pl.ds(n * FF_PAD, A_ROWS)
            total = head_term(part, 3, rows)
            head[rows, lanes] = total
            head_a[n, :, lanes] = total.astype(BF16)
        start_towards(halves, part)

    grds[0].got(*ORDER[3][1])
    send_sums(0)
    grds[1].near()
    add_head(1, 0)
    add_head(1, 1)
    add_head(1, 2)
    grds[1].far()
    far.send(0, 1, 2, 3)
    txt.pass_on()
    txt.near()
    grds[1].got(*ORDER[3][1])
    send_sums(1)

    def settle_late(part):
        for copy in parts[1 + part]:
            copy.wait_recv()
        pair = slice(2 * part, 2 * part + 2)
        total = part_b[z, pair].astype(F32)
        for n in range(7):
            total = total + in_b[n, pair].astype(F32)
        sum_b[pair] = total.astype(BF16)
        start_towards(lates, part)

    visit_images(1, txt)
    visit_images(2, txt)
    settle_late(0)
    txt.far()
    far.pass_on()

    for copy in halves:
        copy.wait_recv()
    total = head[pl.ds(pl.multiple_of(xh * FF_PAD, 16), A_ROWS), window(xl)]
    for n in range(3):
        total = total + head_in[n].astype(F32)
    turned[...] = jnp.transpose(total[0:128])
    row = lax.broadcasted_iota(jnp.int32, (256, 128), 0)
    column = lax.broadcasted_iota(jnp.int32, (256, 128), 1)
    rest = total[128:A_ROWS].astype(BF16)
    for n in range(8):
        rows = pl.ds(pl.multiple_of(n * D_DEV + xl * 64, 8), D_DEV)
        part_a[n, 0:D_DEV] = turned[rows].astype(BF16)
        first = min(n * D_DEV // 128 * 128, LANES - 256)
        shift = n * D_DEV - first + 64 * xl
        pick = jnp.where((row == column + shift) & (column < D_DEV), 1.0, 0.0).astype(BF16)
        part_a[n, 80:96] = jnp.dot(
            rest[:, first : first + 256], pick, preferred_element_type=F32
        ).astype(BF16)
    for copy in parts[0]:
        copy.start()

    settle_late(1)
    far.near()
    visit_images(3, txt)
    visit_images(1, far)
    visit_images(2, far)
    far.far()
    visit_images(3, far)
    image_out[...] = unit_back(image_ref[...].astype(F32), image_sum[...])

    for copy in parts[0]:
        copy.wait_recv()
    total = part_a[z].astype(F32)
    for n in range(7):
        total = total + in_a[n].astype(F32)
    head_out[:, 0:128] = total[0:D_DEV]
    tail = jnp.concatenate([total[80:96], jnp.zeros((112, 128), F32)], axis=0)
    head_out[:, 256:FF_DEV] = jnp.transpose(tail)[0:D_DEV, 0 : FF_DEV - 256]
    for copy in lates:
        copy.wait_recv()
    total = sum_b[2 * xl + xh].astype(F32)
    for n in range(3):
        total = total + far_b[n].astype(F32)
    head_out[:, 128:256] = total[0:D_DEV]

    for gather in (img, txt, far, *grds):
        gather.finish()
    for copy in pieces + halves + lates + parts[0] + parts[1] + parts[2]:
        copy.wait_send()
    for copy in (text_across, text_back):
        copy.wait_send()


def settle(image_ref, head_ref, image_out, head_out):
    image_out[...] = image_ref[...]
    head_out[...] = head_ref[...]


def local(image_emb, text_hidden, head_weight, positive, log_scale, bias):
    vmem = pl.BlockSpec(memory_space=pltpu.VMEM)
    smem = pl.BlockSpec(memory_space=pltpu.SMEM)
    dma = pltpu.SemaphoreType.DMA
    sends = len(SENDS)
    image_grad, head_turned = pl.pallas_call(
        kernel,
        out_shape=(
            jax.ShapeDtypeStruct((ROWS, D), F32),
            jax.ShapeDtypeStruct((D_DEV, FF_DEV), F32),
        ),
        in_specs=[vmem, vmem, pl.BlockSpec(memory_space=pl.ANY), vmem, smem, smem],
        out_specs=(vmem, vmem),
        scratch_shapes=[
            pltpu.VMEM((FF, D), BF16),
            pltpu.VMEM((8, ROWS, D), BF16),
            pltpu.VMEM((8, ROWS, D), BF16),
            pltpu.VMEM((8, ROWS, D), BF16),
            pltpu.VMEM((8, ROWS, D), BF16),
            pltpu.VMEM((ROWS, D), F32),
            pltpu.VMEM((ROWS, D), F32),
            pltpu.VMEM((ROWS, D), F32),
            pltpu.VMEM((ROWS, D), F32),
            pltpu.VMEM((ROWS, D), BF16),
            pltpu.VMEM((ROWS, D), BF16),
            pltpu.VMEM((8, 2 * FF_PAD, ROWS), BF16),
            pltpu.VMEM((4, 2 * FF_PAD, 2 * ROWS), BF16),
            pltpu.VMEM((2 * FF_PAD, D), F32),
            pltpu.VMEM((2, A_ROWS, D), BF16),
            pltpu.VMEM((3, A_ROWS, LANES), BF16),
            pltpu.VMEM((LANES, 128), F32),
            pltpu.VMEM((2, D, 128), F32),
            pltpu.VMEM((8, 96, 128), BF16),
            pltpu.VMEM((8, 4, 80, 128), BF16),
            pltpu.VMEM((7, 96, 128), BF16),
            pltpu.VMEM((7, 4, 80, 128), BF16),
            pltpu.VMEM((4, 80, 128), BF16),
            pltpu.VMEM((3, 80, 128), BF16),
            dma((9,)),
            dma((sends,)),
            dma((sends,)),
            dma((sends,)),
            dma((sends,)),
            dma((sends,)),
            dma((sends,)),
            dma((sends,)),
            dma((sends,)),
            dma((sends,)),
            dma((sends,)),
            dma((2,)),
            dma((2,)),
            dma((7,)),
            dma((7,)),
            dma((6,)),
            dma((6,)),
            dma((21,)),
            dma((21,)),
        ],
        compiler_params=pltpu.CompilerParams(
            collective_id=0, has_side_effects=True, vmem_limit_bytes=60 * 1024 * 1024
        ),
    )(
        image_emb,
        text_hidden.T,
        head_weight,
        positive,
        log_scale,
        bias,
    )
    image_grad, head_turned = pl.pallas_call(
        settle,
        out_shape=(
            jax.ShapeDtypeStruct((ROWS, D), F32),
            jax.ShapeDtypeStruct((D_DEV, FF_DEV), F32),
        ),
        in_specs=[vmem, vmem],
        out_specs=(vmem, vmem),
        compiler_params=pltpu.CompilerParams(vmem_limit_bytes=60 * 1024 * 1024),
    )(image_grad, head_turned)
    return image_grad, head_turned.T


def solution(mesh):
    in_specs = (
        P(("grp", "blk"), None),
        P(("grp", "blk"), None),
        P(),
        P(("grp", "blk"), None),
        P(),
        P(),
    )
    out_specs = (P(("grp", "blk"), None), P("blk", "grp"))
    return jax.shard_map(local, mesh=mesh, in_specs=in_specs, out_specs=out_specs, check_vma=False)
```

```python
import jax
import jax.numpy as jnp
from jax import lax
from jax.experimental import pallas as pl
from jax.experimental.pallas import tpu as pltpu
from jax.sharding import PartitionSpec as P

MESH = pl.DeviceIdType.MESH
BF16 = jnp.bfloat16
F32 = jnp.float32

ROWS = 128
D = 1152
FF = 4304
FF_DEV = 269
FF_PAD = 272
WINDOW = 288
D_DEV = 72
LANES = 640
CHUNK = 512
A_ROWS, B_ROWS = 144, 128
LOW_LANES, HIGH_LANES = (0, LANES), (LANES, D - LANES)


def nt_dot(left, right):
    return lax.dot_general(left, right, (((1,), (1,)), ((), ())), preferred_element_type=F32)


def tn_dot(left, right):
    return lax.dot_general(left, right, (((0,), (0,)), ((), ())), preferred_element_type=F32)


class Place:
    def __init__(self):
        self.g = lax.axis_index("grp")
        self.b = lax.axis_index("blk")
        rest = lax.rem(self.b, 4)
        self.y, self.xh, self.c = lax.div(self.b, 4), lax.div(rest, 2), lax.rem(rest, 2)
        self.xl, self.z = lax.div(self.g, 8), lax.rem(self.g, 8)

    def slot(self, dy, flip_c):
        return self.turn(dy) * 2 + (1 - self.c if flip_c else self.c)

    def turn(self, dy):
        return lax.rem(self.y + dy, 4)

    def device(self, dy=0, flip_c=0, flip_xh=0, flip_xl=0, dz=0):
        c = 1 - self.c if flip_c else self.c
        xh = 1 - self.xh if flip_xh else self.xh
        xl = 1 - self.xl if flip_xl else self.xl
        return (xl * 8 + lax.rem(self.z + dz, 8), self.turn(dy) * 4 + xh * 2 + c)


FULL, LOW, HIGH = (0, ROWS), (0, ROWS // 2), (ROWS // 2, ROWS // 2)
OWN, UP, DOWN, FAR, TWIN = (0, 0), (1, 0), (3, 0), (2, 0), (0, 1)
SENDS = [
    (OWN, LOW, UP, DOWN),
    (OWN, HIGH, DOWN, UP),
    (OWN, HIGH, UP, DOWN),
    (OWN, LOW, DOWN, UP),
    (DOWN, LOW, UP, FAR),
    (UP, HIGH, DOWN, FAR),
    (OWN, FULL, TWIN, TWIN),
    (DOWN, FULL, TWIN, (3, 1)),
    (UP, FULL, TWIN, (1, 1)),
    (FAR, LOW, TWIN, (2, 1)),
    (FAR, HIGH, TWIN, (2, 1)),
]
ORDER = [(0, (6,)), (3, (7,)), (1, (8,)), (2, (9, 10))]


class Gather:
    def __init__(self, place, buf, send_sem, recv_sem, lanes=(0, D)):
        self.place, self.buf, self.send_sem, self.recv_sem = place, buf, send_sem, recv_sem
        self.lanes = pl.ds(*lanes)
        self.held = []

    def copy(self, i, block):
        _, (first, count), target, _ = SENDS[i]
        ref = self.buf.at[self.place.slot(*block), pl.ds(first, count), self.lanes]
        return pltpu.make_async_remote_copy(
            src_ref=ref,
            dst_ref=ref,
            send_sem=self.send_sem.at[i],
            recv_sem=self.recv_sem.at[i],
            device_id=self.place.device(*target),
            device_id_type=MESH,
        )

    def send(self, *which):
        for i in which:
            copy = self.copy(i, SENDS[i][0])
            copy.start()
            self.held.append(copy)

    def got(self, *which):
        for i in which:
            self.copy(i, SENDS[i][3]).wait_recv()

    def pass_on(self):
        self.got(0)
        self.send(4)
        self.got(1)
        self.send(5)

    def near(self):
        self.got(2)
        self.send(7)
        self.got(3)
        self.send(8)

    def far(self):
        self.got(4)
        self.send(9)
        self.got(5)
        self.send(10)

    def finish(self):
        for copy in self.held:
            copy.wait_send()


def kernel(
    image_ref, hidden_ref, weight_ref, positive_ref, scale_ref, bias_ref,
    image_out, head_out,
    weight_buf, images, texts, far_texts, grads, raw, text_sum, image_sum, far_sum,
    text_back_out, text_back_in,
    piece_out, piece_in, head, head_a, head_in, turned, turned_b,
    part_a, part_b, in_a, in_b, sum_b, far_b,
    weight_sem, img_send, img_recv, txt_send, txt_recv, far_send, far_recv,
    low_send, low_recv, high_send, high_recv,
    x_send, x_recv, hid_send, hid_recv, half_send, half_recv, part_send, part_recv,
):
    place = Place()
    y, c, xh, xl, z = place.y, place.c, place.xh, place.xl, place.z
    own = place.slot(*OWN)

    barrier = pltpu.get_barrier_semaphore()
    peers = [place.device(dy, fc) for dy in range(4) for fc in range(2) if dy or fc]
    peers += [place.device(flip_xh=1), place.device(flip_xl=1), place.device(flip_xh=1, flip_xl=1)]
    peers += [place.device(dz=d) for d in range(1, 8)]
    for peer in peers:
        pl.semaphore_signal(barrier, inc=1, device_id=peer, device_id_type=MESH)

    bounds = [(k, min(CHUNK, FF - k)) for k in range(0, FF, CHUNK)]
    weight_copies = []
    for n, (first, count) in enumerate(bounds):
        rows = pl.ds(first, count)
        copy = pltpu.make_async_copy(weight_ref.at[rows], weight_buf.at[rows], weight_sem.at[n])
        copy.start()
        weight_copies.append(copy)

    def unit_of(values):
        norm = jnp.sqrt(jnp.sum(values * values, axis=-1, keepdims=True) + 1e-06)
        return norm, values / norm

    def unit_back(values, incoming):
        norm, direction = unit_of(values)
        along = jnp.sum(direction * incoming, axis=-1, keepdims=True)
        return (incoming - direction * along) / norm

    def remote(src, dst, send_sem, recv_sem, target):
        return pltpu.make_async_remote_copy(
            src_ref=src,
            dst_ref=dst,
            send_sem=send_sem,
            recv_sem=recv_sem,
            device_id=target,
            device_id_type=MESH,
        )

    img = Gather(place, images, img_send, img_recv)
    txt = Gather(place, texts, txt_send, txt_recv)
    far = Gather(place, far_texts, far_send, far_recv)
    grds = [
        Gather(place, grads, low_send, low_recv, LOW_LANES),
        Gather(place, grads, high_send, high_recv, HIGH_LANES),
    ]
    partner = place.device(flip_xh=1)

    def across(n, src, dst):
        return remote(src, dst, x_send.at[n], x_recv.at[n], partner)

    text_across = across(0, texts.at[own], far_texts.at[own])
    text_back = across(1, text_back_out, text_back_in)

    def cut(start, first, window):
        row = lax.broadcasted_iota(jnp.int32, (FF_PAD, window), 0)
        column = lax.broadcasted_iota(jnp.int32, (FF_PAD, window), 1)
        wanted = jnp.where(row < 128, row, jnp.where(row < A_ROWS, row + 128, row - 16))
        pick = jnp.where(column == wanted + (start - first), 1.0, 0.0).astype(BF16)
        return jnp.dot(
            pick, hidden_ref[pl.ds(first, window)], preferred_element_type=F32
        ).astype(BF16)

    def cut_step(n, carry):
        start = n * FF_DEV
        first = pl.multiple_of(lax.div(start, 16) * 16, 16)
        column, half = lax.div(n, 4) * 2 + lax.rem(n, 2), lax.rem(lax.div(n, 2), 2)
        rows = pl.ds(pl.multiple_of(half * FF_PAD, 16), FF_PAD)
        piece_out[column, rows] = cut(start, first, WINDOW)
        return carry

    images[own] = unit_of(image_ref[...].astype(F32))[1].astype(BF16)
    lax.fori_loop(0, 5, cut_step, 0)
    pl.semaphore_wait(barrier, len(peers))
    img.send(0, 1, 6)
    lax.fori_loop(5, 11, cut_step, 0)
    img.send(2, 3)
    lax.fori_loop(11, 15, cut_step, 0)
    last = 15 * FF_DEV
    piece_out[7, FF_PAD : 2 * FF_PAD] = cut(last, last // 16 * 16, FF - last // 16 * 16)

    for n, (first, count) in enumerate(bounds):
        weight_copies[n].wait()
        rows = pl.ds(first, count)
        term = tn_dot(hidden_ref[rows], weight_buf[rows])
        raw[...] = term if n == 0 else raw[...] + term
    texts[own] = unit_of(raw[...])[1].astype(BF16)
    text_across.start()
    txt.send(6)
    img.pass_on()

    def lane(core):
        return pl.ds(pl.multiple_of(core * ROWS, ROWS), ROWS)

    OTHERS = [(dy, fc) for dy in (1, 3, 2) for fc in range(2)] + [TWIN]

    def piece_copy(n, dy, fc, back=False):
        if back:
            dst = piece_in.at[place.turn(4 - dy), :, lane(1 - c if fc else c)]
        else:
            dst = piece_in.at[y, :, lane(c)]
        return remote(
            piece_out.at[place.slot(dy, fc)], dst, hid_send.at[n], hid_recv.at[n],
            place.device(dy, fc),
        )

    pieces = [piece_copy(n, *target) for n, target in enumerate(OTHERS)]
    piece_in[y, :, lane(c)] = piece_out[own]
    img.near()
    for copy in pieces:
        copy.start()

    logit_scale = jnp.exp(jnp.full((1, 2 * ROWS), scale_ref[0], F32))
    logit_bias = bias_ref[0]
    text_row = lax.broadcasted_iota(jnp.int32, (ROWS, ROWS), 0)
    label = jnp.where(text_row == positive_ref[...], 1.0, 0.0)

    def with_twin(value):
        return jnp.concatenate(
            [jnp.where(c == 0, value, 0.0), jnp.where(c == 0, 0.0, value)], axis=1
        )

    def chip(buf, dy):
        return buf[pl.ds(2 * place.turn(dy), 2)].reshape(2 * ROWS, D)

    def visit(unit, block, total, first, own_label=None):
        chance = jax.nn.sigmoid(logit_scale * nt_dot(unit, block) + logit_bias)
        if own_label is not None:
            chance = chance - with_twin(own_label)
        weight = (logit_scale * chance).astype(BF16)
        term = jnp.dot(weight, block, preferred_element_type=F32)
        total[...] = term if first else total[...] + term

    def visit_texts(n):
        label_of = label if n == 0 else None
        visit(texts[own], chip(images, ORDER[n][0]), text_sum, n == 0, label_of)

    def visit_far_texts(n):
        visit(far_texts[own], chip(images, ORDER[n][0]), far_sum, n == 0)

    def visit_images(n, gather):
        gather.got(*ORDER[n][1])
        own_label = jnp.transpose(label) if n == 0 and gather is txt else None
        block = chip(gather.buf, ORDER[n][0])
        visit(images[own], block, image_sum, own_label is not None, own_label)

    img.far()
    for n in range(3):
        img.got(*ORDER[n][1])
        visit_texts(n)
    text_across.wait_recv()
    far.send(6)
    for n in range(3):
        visit_far_texts(n)
    img.got(*ORDER[3][1])
    visit_far_texts(3)
    text_back_out[...] = far_sum[...].astype(BF16)
    text_back.start()
    txt.send(0, 1, 2, 3)
    visit_texts(3)
    visit_images(0, txt)
    visit_images(0, far)
    text_back.wait_recv()
    incoming = text_sum[...] + text_back_in[...].astype(F32)
    grads[own] = unit_back(raw[...], incoming).astype(BF16)
    grds[0].send(0, 1, 2, 3, 6)
    for n, (dy, fc) in enumerate(OTHERS):
        piece_copy(n, dy, fc, back=True).wait_recv()

    def head_term(part, n, rows):
        first, count = (LOW_LANES, HIGH_LANES)[part]
        lanes = pl.ds(first, count)
        turn = place.turn(ORDER[n][0])
        block = grads[pl.ds(2 * turn, 2), :, lanes].reshape(2 * ROWS, count)
        term = jnp.dot(piece_in[turn, rows], block, preferred_element_type=F32)
        return term if n == 0 else head[rows, lanes] + term

    def add_head(part, n):
        grds[part].got(*ORDER[n][1])
        head[:, pl.ds(*(LOW_LANES, HIGH_LANES)[part])] = head_term(part, n, pl.ds(0, 2 * FF_PAD))

    add_head(0, 0)
    grds[0].pass_on()
    grds[1].send(0, 1, 2, 3, 6)
    grds[0].near()
    add_head(0, 1)
    add_head(0, 2)
    grds[1].pass_on()
    grds[0].far()

    FLIPS = [(0, 1), (1, 0), (1, 1)]
    ROUND = (1, 7, 2, 6, 3, 5, 4)

    def window(half):
        return pl.ds(pl.multiple_of(half * 512, 128), LANES)

    def half_copy(n, flip_xh, flip_xl):
        to_xh = 1 - xh if flip_xh else xh
        to_xl = 1 - xl if flip_xl else xl
        return remote(
            head_a.at[to_xh, :, window(to_xl)], head_in.at[n], half_send.at[n], half_recv.at[n],
            place.device(flip_xh=flip_xh, flip_xl=flip_xl),
        )

    def late_copy(n, flip_xh, flip_xl):
        to_xh = 1 - xh if flip_xh else xh
        to_xl = 1 - xl if flip_xl else xl
        return remote(
            sum_b.at[2 * to_xl + to_xh], far_b.at[n], half_send.at[3 + n], half_recv.at[3 + n],
            place.device(flip_xh=flip_xh, flip_xl=flip_xl),
        )

    def part_copy(d, part):
        target = lax.rem(z + d, 8)
        if part == 0:
            src, dst = part_a.at[target], in_a.at[d - 1]
        else:
            pair = pl.ds(2 * (part - 1), 2)
            src, dst = part_b.at[target, pair], in_b.at[d - 1, pair]
        n = part * 7 + d - 1
        return remote(src, dst, part_send.at[n], part_recv.at[n], place.device(dz=d))

    halves = [half_copy(n, *flips) for n, flips in enumerate(FLIPS)]
    lates = [late_copy(n, *flips) for n, flips in enumerate(FLIPS)]
    parts = [[part_copy(d, part) for d in ROUND] for part in range(3)]

    def start_towards(copies, half):
        for copy, (_, flip_xl) in zip(copies, FLIPS):
            to_xl = 1 - xl if flip_xl else xl
            pl.when(to_xl == half)(copy.start)

    def send_sums(part):
        first, count = (LOW_LANES, HIGH_LANES)[part]
        lanes = pl.ds(first, count)
        for n in range(2):
            rows = pl.ds(n * FF_PAD + A_ROWS, B_ROWS)
            turned_b[n, lanes] = jnp.transpose(head_term(part, 3, rows))
            for k in range(8):
                begin = (8 * part + k) * D_DEV
                part_b[k, 2 * part + n, 0:D_DEV] = turned_b[n, begin : begin + D_DEV].astype(BF16)
        for copy in parts[1 + part]:
            copy.start()
        for n in range(2):
            rows = pl.ds(n * FF_PAD, A_ROWS)
            total = head_term(part, 3, rows)
            head[rows, lanes] = total
            head_a[n, :, lanes] = total.astype(BF16)
        start_towards(halves, part)

    grds[0].got(*ORDER[3][1])
    send_sums(0)
    grds[1].near()
    add_head(1, 0)
    add_head(1, 1)
    add_head(1, 2)
    grds[1].far()
    far.send(0, 1, 2, 3)
    txt.pass_on()
    txt.near()
    grds[1].got(*ORDER[3][1])
    send_sums(1)

    def settle_late(part):
        for copy in parts[1 + part]:
            copy.wait_recv()
        pair = slice(2 * part, 2 * part + 2)
        total = part_b[z, pair].astype(F32)
        for n in range(7):
            total = total + in_b[n, pair].astype(F32)
        sum_b[pair] = total.astype(BF16)
        start_towards(lates, part)

    visit_images(1, txt)
    visit_images(2, txt)
    settle_late(0)
    txt.far()
    far.pass_on()

    for copy in halves:
        copy.wait_recv()
    total = head[pl.ds(pl.multiple_of(xh * FF_PAD, 16), A_ROWS), window(xl)]
    for n in range(3):
        total = total + head_in[n].astype(F32)
    turned[...] = jnp.transpose(total[0:128])
    row = lax.broadcasted_iota(jnp.int32, (256, 128), 0)
    column = lax.broadcasted_iota(jnp.int32, (256, 128), 1)
    rest = total[128:A_ROWS].astype(BF16)
    for n in range(8):
        rows = pl.ds(pl.multiple_of(n * D_DEV + xl * 64, 8), D_DEV)
        part_a[n, 0:D_DEV] = turned[rows].astype(BF16)
        first = min(n * D_DEV // 128 * 128, LANES - 256)
        shift = n * D_DEV - first + 64 * xl
        pick = jnp.where((row == column + shift) & (column < D_DEV), 1.0, 0.0).astype(BF16)
        part_a[n, 80:96] = jnp.dot(
            rest[:, first : first + 256], pick, preferred_element_type=F32
        ).astype(BF16)
    for copy in parts[0]:
        copy.start()

    settle_late(1)
    far.near()
    visit_images(3, txt)
    visit_images(1, far)
    visit_images(2, far)
    far.far()
    visit_images(3, far)
    image_out[...] = unit_back(image_ref[...].astype(F32), image_sum[...])

    for copy in parts[0]:
        copy.wait_recv()
    total = part_a[z].astype(F32)
    for n in range(7):
        total = total + in_a[n].astype(F32)
    head_out[:, 0:128] = total[0:D_DEV]
    tail = jnp.concatenate([total[80:96], jnp.zeros((112, 128), F32)], axis=0)
    head_out[:, 256:FF_DEV] = jnp.transpose(tail)[0:D_DEV, 0 : FF_DEV - 256]
    for copy in lates:
        copy.wait_recv()
    total = sum_b[2 * xl + xh].astype(F32)
    for n in range(3):
        total = total + far_b[n].astype(F32)
    head_out[:, 128:256] = total[0:D_DEV]

    for gather in (img, txt, far, *grds):
        gather.finish()
    for copy in pieces + halves + lates + parts[0] + parts[1] + parts[2]:
        copy.wait_send()
    for copy in (text_across, text_back):
        copy.wait_send()


def settle(image_ref, head_ref, image_out, head_out):
    image_out[...] = image_ref[...]
    head_out[...] = head_ref[...]


def local(image_emb, text_hidden, head_weight, positive, log_scale, bias):
    vmem = pl.BlockSpec(memory_space=pltpu.VMEM)
    smem = pl.BlockSpec(memory_space=pltpu.SMEM)
    dma = pltpu.SemaphoreType.DMA
    sends = len(SENDS)
    image_grad, head_turned = pl.pallas_call(
        kernel,
        out_shape=(
            jax.ShapeDtypeStruct((ROWS, D), F32),
            jax.ShapeDtypeStruct((D_DEV, FF_DEV), F32),
        ),
        in_specs=[vmem, vmem, pl.BlockSpec(memory_space=pl.ANY), vmem, smem, smem],
        out_specs=(vmem, vmem),
        scratch_shapes=[
            pltpu.VMEM((FF, D), BF16),
            pltpu.VMEM((8, ROWS, D), BF16),
            pltpu.VMEM((8, ROWS, D), BF16),
            pltpu.VMEM((8, ROWS, D), BF16),
            pltpu.VMEM((8, ROWS, D), BF16),
            pltpu.VMEM((ROWS, D), F32),
            pltpu.VMEM((ROWS, D), F32),
            pltpu.VMEM((ROWS, D), F32),
            pltpu.VMEM((ROWS, D), F32),
            pltpu.VMEM((ROWS, D), BF16),
            pltpu.VMEM((ROWS, D), BF16),
            pltpu.VMEM((8, 2 * FF_PAD, ROWS), BF16),
            pltpu.VMEM((4, 2 * FF_PAD, 2 * ROWS), BF16),
            pltpu.VMEM((2 * FF_PAD, D), F32),
            pltpu.VMEM((2, A_ROWS, D), BF16),
            pltpu.VMEM((3, A_ROWS, LANES), BF16),
            pltpu.VMEM((LANES, 128), F32),
            pltpu.VMEM((2, D, 128), F32),
            pltpu.VMEM((8, 96, 128), BF16),
            pltpu.VMEM((8, 4, 80, 128), BF16),
            pltpu.VMEM((7, 96, 128), BF16),
            pltpu.VMEM((7, 4, 80, 128), BF16),
            pltpu.VMEM((4, 80, 128), BF16),
            pltpu.VMEM((3, 80, 128), BF16),
            dma((9,)),
            dma((sends,)),
            dma((sends,)),
            dma((sends,)),
            dma((sends,)),
            dma((sends,)),
            dma((sends,)),
            dma((sends,)),
            dma((sends,)),
            dma((sends,)),
            dma((sends,)),
            dma((2,)),
            dma((2,)),
            dma((7,)),
            dma((7,)),
            dma((6,)),
            dma((6,)),
            dma((21,)),
            dma((21,)),
        ],
        compiler_params=pltpu.CompilerParams(
            collective_id=0, has_side_effects=True, vmem_limit_bytes=60 * 1024 * 1024
        ),
    )(
        image_emb,
        text_hidden.T,
        head_weight,
        positive,
        log_scale,
        bias,
    )
    image_grad, head_turned = pl.pallas_call(
        settle,
        out_shape=(
            jax.ShapeDtypeStruct((ROWS, D), F32),
            jax.ShapeDtypeStruct((D_DEV, FF_DEV), F32),
        ),
        in_specs=[vmem, vmem],
        out_specs=(vmem, vmem),
        compiler_params=pltpu.CompilerParams(vmem_limit_bytes=60 * 1024 * 1024),
    )(image_grad, head_turned)
    return image_grad, head_turned.T


def solution(mesh):
    in_specs = (
        P(("grp", "blk"), None),
        P(("grp", "blk"), None),
        P(),
        P(("grp", "blk"), None),
        P(),
        P(),
    )
    out_specs = (P(("grp", "blk"), None), P("blk", "grp"))
    return jax.shard_map(local, mesh=mesh, in_specs=in_specs, out_specs=out_specs, check_vma=False)
```
